512 devices in a mesh: frame: 64 (over z_hi, x, y), ref: 8 (over z_lo, core).
Axes of the slice: x: 4, y: 4, z: 16 (z_hi: 4, z_lo: 4; z = z_hi * 4 + z_lo), core: 2. Of those that a mesh axis runs over, the one named last changes fastest.
Arguments:
- queries: bfloat16 [16384, 2048], P('frame', 'ref'), may hold values from -1.6953125 to 1.6953125
- keys: bfloat16 [16384, 2048], P('frame', 'ref'), may hold values from -1.6953125 to 1.6953125
- values: bfloat16 [16384, 2048], P('frame', 'ref'), may hold values from -6 to 6
- out_grad: bfloat16 [16384, 2048], P('frame', 'ref'), may hold values from -24 to 24
- ref_keys: bfloat16 [1024, 2048], P('ref'), may hold values from -1.6953125 to 1.6953125
- ref_values: bfloat16 [1024, 2048], P('ref'), may hold values from -6 to 6
- frame_weight: float32 [64], P('frame'), may hold values from 0.5 to 12, as said below
Outputs:
- grad_queries: bfloat16 [16384, 2048], P('frame', 'ref')
- grad_keys: bfloat16 [16384, 2048], P('frame', 'ref')
- grad_values: bfloat16 [16384, 2048], P('frame', 'ref')
- grad_ref_keys: float32 [1024, 2048], P('frame', 'ref')
- grad_ref_values: float32 [1024, 2048], P('frame', 'ref')
The draws below stay inside these ranges and needn't reach their ends.
Inputs may be any that keep to these rules, and one draw needn't show every extreme that they name: `frame_weight`: positive loss weight of each frame.
All inputs are finite; a program needn't handle non-finite values.
Results may differ from the reference program's by a relative error of at most 0.005.
Values may be sent and summed in bfloat16 or wider, within the bound.
A program may use at most 64 MiB of HBM per device.

```python
import jax
import jax.numpy as jnp
from jax import lax

HEAD_DIM = 64
HEADS = 32
WIDTH = 2048
SEQ = 256
REFS = 1024
FRAMES = 64
TOKENS = 16384


def draw_frame_weight(key, part):
    key = jax.random.fold_in(key, 11)
    position = jnp.arange(FRAMES, dtype=jnp.float32) / (FRAMES - 1)
    return 3.0 ** position * jax.random.uniform(key, (FRAMES,), jnp.float32, 0.7, 1.4)


def levels(own_key, dims, shards, least, largest):
    def one(dim, parts):
        heights = jax.random.uniform(jax.random.fold_in(jax.random.fold_in(own_key, 6), dim), (parts,), jnp.float32, least / len(shards), largest / len(shards))
        return jnp.repeat(jnp.exp(heights), dims[dim] // parts).reshape((-1,) + (1,) * (len(dims) - dim - 1))

    factor_of = one(*shards[0])
    for cut in shards[1:]:
        factor_of = factor_of * one(*cut)
    return factor_of


def noise(own_key, dims, deviation, most, split=(), kind=jnp.bfloat16):
    loudness = levels(own_key, dims, split, -0.22, 0.18) if split else 1.0
    values = jax.random.normal(own_key, dims, jnp.float32) * deviation * loudness
    return jnp.minimum(jnp.maximum(values, -most), most).astype(kind)


def setup_inputs(seed: int = 0) -> dict:
    key_list = jax.random.split(jax.random.key(seed), 8)
    queries = jnp.clip(jax.random.uniform(key_list[0], (TOKENS, WIDTH), jnp.float32, -1.6953125, 1.6953125) * levels(key_list[0], (TOKENS, WIDTH), ((0, 64), (1, 8)), -0.4, 0.0), -1.6953125, 1.6953125).astype(jnp.bfloat16)
    keys = jnp.clip(jax.random.uniform(key_list[1], (TOKENS, WIDTH), jnp.float32, -1.6953125, 1.6953125) * levels(key_list[1], (TOKENS, WIDTH), ((0, 64), (1, 8)), -0.4, 0.0), -1.6953125, 1.6953125).astype(jnp.bfloat16)
    values = noise(key_list[2], (TOKENS, WIDTH), 1.0, 6.0, ((0, 64), (1, 8)))
    out_grad = noise(key_list[3], (TOKENS, WIDTH), 4.0, 24.0, ((0, 64), (1, 8)))
    ref_keys = jnp.clip(jax.random.uniform(key_list[4], (REFS, WIDTH), jnp.float32, -1.6953125, 1.6953125) * levels(key_list[4], (REFS, WIDTH), ((0, 8),), -0.4, 0.0), -1.6953125, 1.6953125).astype(jnp.bfloat16)
    ref_values = noise(key_list[5], (REFS, WIDTH), 1.0, 6.0, ((0, 8),))
    frame_weight = draw_frame_weight(jax.random.fold_in(key_list[7], 71), 0)
    return dict(queries=queries, keys=keys, values=values, out_grad=out_grad, ref_keys=ref_keys, ref_values=ref_values, frame_weight=frame_weight)


def head_grads(query_rows, key_self, value_self, grad_out, key_ref, value_ref, softmax_scale):
    length = query_rows.shape[0]
    all_keys = jnp.concatenate([key_self, key_ref], 0)
    all_values = jnp.concatenate([value_self, value_ref], 0)
    scores = jnp.dot(query_rows, all_keys.T, preferred_element_type=jnp.float32) * softmax_scale
    raised = jnp.exp(scores)
    shares = raised / jnp.sum(raised, axis=1, keepdims=True)
    shares_low = shares.astype(jnp.bfloat16)
    attended = jnp.dot(shares_low, all_values, preferred_element_type=jnp.float32)
    inner_term = jnp.sum(grad_out.astype(jnp.float32) * attended, axis=1, keepdims=True)
    grad_shares = jnp.dot(grad_out, all_values.T, preferred_element_type=jnp.float32)
    grad_scores = (shares * (grad_shares - inner_term)).astype(jnp.bfloat16)
    grad_query = jnp.dot(grad_scores, all_keys, preferred_element_type=jnp.float32) * softmax_scale
    grad_key = jnp.dot(grad_scores[:, :length].T, query_rows, preferred_element_type=jnp.float32) * softmax_scale
    grad_value = jnp.dot(shares_low[:, :length].T, grad_out, preferred_element_type=jnp.float32)
    return grad_query, grad_key, grad_value, grad_scores[:, length:], shares_low[:, length:]


def ref_partial(ref_scores, ref_shares, query_rows, grad_out, softmax_scale):
    part_key = jnp.dot(ref_scores.T, query_rows, preferred_element_type=jnp.float32) * softmax_scale
    part_value = jnp.dot(ref_shares.T, grad_out, preferred_element_type=jnp.float32)
    return part_key, part_value


def reference(queries, keys, values, out_grad, ref_keys, ref_values, frame_weight):
    softmax_scale = HEAD_DIM ** -0.5
    normed_weight = frame_weight * FRAMES / jnp.sum(frame_weight)

    def split_frames(array):
        return array.reshape(FRAMES, SEQ, HEADS, HEAD_DIM).transpose(0, 2, 1, 3)

    def join_frames(array):
        return array.transpose(0, 2, 1, 3).reshape(TOKENS, WIDTH)

    key_heads = ref_keys.reshape(REFS, HEADS, HEAD_DIM).transpose(1, 0, 2)
    value_heads = ref_values.reshape(REFS, HEADS, HEAD_DIM).transpose(1, 0, 2)

    def one_head(items):
        query_rows, key_self, value_self, grad_out, key_ref, value_ref = items
        grad_query, grad_key, grad_value, ref_scores, ref_shares = head_grads(
            query_rows, key_self, value_self, grad_out, key_ref, value_ref, softmax_scale)
        part_key, part_value = ref_partial(ref_scores, ref_shares, query_rows, grad_out, softmax_scale)
        return grad_query, grad_key, grad_value, part_key, part_value

    def frame_step(carry, items):
        query_frame, key_frame, value_frame, grad_frame, weight_now = items
        grad_query, grad_key, grad_value, part_key, part_value = lax.map(
            one_head, (query_frame, key_frame, value_frame, grad_frame, key_heads, value_heads))
        carry = (carry[0] + weight_now * part_key, carry[1] + weight_now * part_value)
        return carry, ((weight_now * grad_query).astype(jnp.bfloat16),
                       (weight_now * grad_key).astype(jnp.bfloat16),
                       (weight_now * grad_value).astype(jnp.bfloat16))

    start_sums = (jnp.zeros((HEADS, REFS, HEAD_DIM), jnp.float32), jnp.zeros((HEADS, REFS, HEAD_DIM), jnp.float32))
    sums, grads = lax.scan(frame_step, start_sums, (split_frames(queries), split_frames(keys), split_frames(values), split_frames(out_grad), normed_weight))
    grad_ref_keys = sums[0].transpose(1, 0, 2).reshape(REFS, WIDTH)
    grad_ref_values = sums[1].transpose(1, 0, 2).reshape(REFS, WIDTH)
    return join_frames(grads[0]), join_frames(grads[1]), join_frames(grads[2]), grad_ref_keys, grad_ref_values
```

```python
import jax
import jax.numpy as jnp
from jax import lax
from jax.experimental import pallas as pl
from jax.experimental.pallas import tpu as pltpu
from jax.sharding import PartitionSpec as P

F32, BF = jnp.float32, jnp.bfloat16
MESH = pl.DeviceIdType.MESH
SCALE = 0.125
EXP2_SCALE = SCALE * 1.4426950408889634
SEQ, WIDTH, PAIR = 256, 256, 128
FRAMES = 64
KEY, VALUE = 0, 1


def dot(a, b):
    return lax.dot_general(a, b, (((1,), (0,)), ((), ())), preferred_element_type=F32)


def fold(a):
    return jnp.sum(a.reshape(-1, 8, a.shape[-1]), axis=0)


def split_heads(p, a, stacked, across):
    a = a[:, PAIR * p : PAIR * (p + 1)]
    low = lax.broadcasted_iota(jnp.int32, (SEQ, PAIR), 1) < 64
    zero = jnp.zeros((SEQ, PAIR), BF)
    stacked[p, 0:SEQ] = jnp.where(low, a, zero)
    stacked[p, SEQ:] = jnp.where(low, zero, a)
    turned = a.T
    top = lax.broadcasted_iota(jnp.int32, (PAIR, SEQ), 0) < 64
    zero = jnp.zeros((PAIR, SEQ), BF)
    across[p, :, 0:SEQ] = jnp.where(top, turned, zero)
    across[p, :, SEQ:] = jnp.where(top, zero, turned)


def kernel(
    q_in, k_in, v_in, d_in, rk_in, rv_in, w_in,
    gq_out, gk_out, gv_out, grk_out, grv_out,
    own, refs, stacked, across, raised, gshare, gscore, gq_t, gkv, result,
    part, got1, part2, got2, part3, got3, weights, weights_got, refout,
    loc_sem, out_sem, zs, zr, cs, cr, gs, gr, s1, r1, s2, r2, s3, r3, ws, wr,
):
    frame, ref = lax.axis_index("frame"), lax.axis_index("ref")
    zhi, x, y = frame // 16, (frame // 4) % 4, frame % 4
    zlo, core = ref // 2, ref % 2

    def at(dx=0, dy=0, dz=0, c=core):
        z = (zhi * 4 + zlo + dz + 16) % 16
        return (((z // 4) * 4 + (x + dx) % 4) * 4 + (y + dy) % 4, (z % 4) * 2 + c)

    near = [at(c=1 - core)]
    near += [at(dz=dz, c=c) for dz in (1, -1, 2, -2) for c in (0, 1)]
    near += [at(dx=o) for o in (1, 2, 3)] + [at(dy=o) for o in (1, 2, 3)]
    near += [at(dz=4 * o) for o in (1, 2, 3)]
    barrier = pltpu.get_barrier_semaphore()
    for device in near:
        pl.semaphore_signal(barrier, inc=1, device_id=device, device_id_type=MESH)

    def columns(r, h):
        return pl.ds(pl.multiple_of(r * WIDTH + h * PAIR, PAIR), PAIR)

    local = []
    for i, a in enumerate((q_in, d_in, k_in, v_in)):
        local.append(pltpu.make_async_copy(a, own.at[i], loc_sem.at[i]))
    ref_in = (rk_in, rv_in)
    local_ref = [
        [pltpu.make_async_copy(ref_in[t].at[:, :, columns(ref, h)], refs.at[t, h, 0, core], loc_sem.at[4 + 2 * h + t]) for t in (0, 1)]
        for h in (0, 1)
    ]
    for copy in local + local_ref[0] + local_ref[1]:
        copy.start()
    weight = w_in[0]
    weights[0] = jnp.full((8, 128), weight, F32)
    pl.semaphore_wait(barrier, len(near))

    sent = []

    def send(src, dst, send_sem, recv_sem, device):
        copy = pltpu.make_async_remote_copy(src, dst, send_sem, recv_sem, device_id=device, device_id_type=MESH)
        copy.start()
        sent.append(copy)

    def arrived(region, sem, any_send_sem):
        pltpu.make_async_remote_copy(region, region, any_send_sem, sem, device_id=at(dx=1), device_id_type=MESH).wait_recv()

    quarter = (x, y)
    for h in (0, 1):
        for t in (0, 1):
            for i, dz in enumerate((1, -1, 2 if t == 0 else -2)):
                slot = (3, 1, 2)[i]
                for c in (0, 1):
                    target = at(dz=dz, c=c)
                    here = ref_in[t].at[quarter[t], :, columns(target[1], h)]
                    send(here, refs.at[t, h, slot, core, quarter[t]], zs.at[h, t, i, c], zr.at[h, t], target)
        for t in (0, 1):
            here = ref_in[t].at[:, :, columns(zlo * 2 + 1 - core, h)]
            send(here, refs.at[t, h, 0, core], cs.at[h, t], cr.at[h, t], at(c=1 - core))
    for o in (1, 2, 3):
        send(weights.at[0], weights_got.at[0, o - 1], ws.at[0, o - 1], wr.at[0, o - 1], at(dx=o))

    def gather_planes(h):
        for t in (0, 1):
            mine = refs.at[t, h, 1:4, :, quarter[t]]
            arrived(mine, zr.at[h, t], zs.at[0, 0, 0, 0])
            for o in (1, 2, 3):
                send(mine, mine, gs.at[h, t, o - 1], gr.at[h, t, o - 1], at(dx=o) if t == 0 else at(dy=o))

    def scores(p, j, keys, values):
        e = jnp.exp2(dot(keys, across[0, p]) * EXP2_SCALE)
        g = dot(values, across[1, p])
        raised[p, j] = e
        gshare[p, j] = g
        return fold(e), fold(e * g)

    def ref_chunk(t, p, s):
        return refs[t, p, s].reshape(SEQ, PAIR)

    def own_chunk(i, p):
        return own[i, :, PAIR * p : PAIR * (p + 1)]

    local[0].wait()
    local[1].wait()
    for p in (0, 1):
        split_heads(p, own[0], stacked.at[0], across.at[0])
        split_heads(p, own[1], stacked.at[1], across.at[1])
    gather_planes(0)
    local[2].wait()
    local[3].wait()
    totals = [None, None]

    def add(p, more):
        totals[p] = more if totals[p] is None else (totals[p][0] + more[0], totals[p][1] + more[1])

    add(0, scores(0, 4, own_chunk(2, 0), own_chunk(3, 0)))
    gather_planes(1)
    add(1, scores(1, 4, own_chunk(2, 1), own_chunk(3, 1)))
    for h in (0, 1):
        for t in (0, 1):
            local_ref[h][t].wait()
            arrived(refs.at[t, h, 0, 1 - core], cr.at[h, t], cs.at[0, 0])
        add(h, scores(h, 0, ref_chunk(0, h, 0), ref_chunk(1, h, 0)))

    def weight_stage(stage):
        for o in (1, 2, 3):
            arrived(weights_got.at[stage, o - 1], wr.at[stage, o - 1], ws.at[0, 0])
        weights[stage + 1] = weights[stage] + weights_got[stage, 0] + weights_got[stage, 1] + weights_got[stage, 2]
        if stage < 2:
            for o in (1, 2, 3):
                target = at(dy=o) if stage == 0 else at(dz=4 * o)
                send(weights.at[stage + 1], weights_got.at[stage + 1, o - 1], ws.at[stage + 1, o - 1], wr.at[stage + 1, o - 1], target)

    weight_stage(0)

    def shares(p, j, norm):
        share = raised[p, j] * norm[0]
        score = (share * (gshare[p, j] - norm[1])).astype(BF)
        gscore[p, j] = score
        return dot(score, stacked[0, p]), dot(share.astype(BF), stacked[1, p])

    norms = [None, None]

    def partial_grads(p):
        for t in (0, 1):
            for o in (1, 2, 3):
                arrived(refs.at[t, p, 1:4, :, (quarter[t] + 4 - o) % 4], gr.at[p, t, o - 1], gs.at[0, 0, 0])
        for s in (1, 2, 3):
            add(p, scores(p, s, ref_chunk(0, p, s), ref_chunk(1, p, s)))
        norm = 1.0 / jnp.sum(totals[p][0], axis=0, keepdims=True)
        norms[p] = (norm, jnp.sum(totals[p][1], axis=0, keepdims=True) * norm)
        for s in range(4):
            for t, grad in enumerate(shares(p, s, norms[p])):
                part[t, p, s] = (grad * weight).astype(BF).reshape(4, 4, 16, PAIR)
        for o in (1, 2, 3):
            send(part.at[0, p, :, (x + o) % 4], got1.at[0, p, o - 1], s1.at[0, p, o - 1], r1.at[0, p, o - 1], at(dx=o))
            send(part.at[1, p, :, :, (y + o) % 4], got1.at[1, p, o - 1], s1.at[1, p, o - 1], r1.at[1, p, o - 1], at(dy=o))

    def total(first, got):
        return first.astype(F32) + got[0].astype(F32) + got[1].astype(F32) + got[2].astype(F32)

    def second_stage(p):
        for t in (0, 1):
            for o in (1, 2, 3):
                arrived(got1.at[t, p, o - 1], r1.at[t, p, o - 1], s1.at[0, 0, 0])
            mine = part[0, p, :, x] if t == 0 else part[1, p, :, :, y]
            part2[t, p] = total(mine, got1.at[t, p]).astype(BF)
            place, device = (y, lambda o: at(dy=o)) if t == 0 else (x, lambda o: at(dx=o))
            for o in (1, 2, 3):
                send(part2.at[t, p, :, (place + o) % 4], got2.at[t, p, o - 1], s2.at[t, p, o - 1], r2.at[t, p, o - 1], device(o))

    def third_stage(p):
        for t in (0, 1):
            for o in (1, 2, 3):
                arrived(got2.at[t, p, o - 1], r2.at[t, p, o - 1], s2.at[0, 0, 0])
            part3[t, p] = total(part2[t, p, :, y if t == 0 else x], got2.at[t, p]).astype(BF)
            for o in (1, 2, 3):
                slot = (zhi + o - zlo + 4) % 4
                send(part3.at[t, p, slot], got3.at[t, p, o - 1], s3.at[t, p, o - 1], r3.at[t, p, o - 1], at(dz=4 * o))

    def frame_grads(p):
        gk, gv = shares(p, 4, norms[p])
        gkv[0, p] = gk
        gkv[1, p] = gv
        sums = [None, None]
        for j in range(5):
            turned = (own_chunk(2, p) if j == 4 else ref_chunk(0, p, j)).T
            for a in (0, 1):
                more = dot(turned[64 * a : 64 * (a + 1)], gscore[p, j, :, SEQ * a : SEQ * (a + 1)])
                sums[a] = more if sums[a] is None else sums[a] + more
        gq_t[p, 0:64] = sums[0]
        gq_t[p, 64:128] = sums[1]

    partial_grads(0)
    partial_grads(1)
    second_stage(0)
    weight_stage(1)
    frame_grads(0)
    second_stage(1)
    third_stage(0)
    frame_grads(1)
    third_stage(1)

    weight_stage(2)
    factor = FRAMES / weights[3, 0:1, 0:1]
    own_factor = weight * factor
    for p in (0, 1):
        cols = slice(PAIR * p, PAIR * (p + 1))
        result[0, :, cols] = (gq_t[p].T * (own_factor * SCALE)).astype(BF)
        result[1, :, cols] = (gkv[0, p] * (own_factor * SCALE)).astype(BF)
        result[2, :, cols] = (gkv[1, p] * own_factor).astype(BF)
    out = [pltpu.make_async_copy(result.at[i], a, out_sem.at[i]) for i, a in enumerate((gq_out, gk_out, gv_out))]
    for copy in out:
        copy.start()
    for p in (0, 1):
        for t in (0, 1):
            for o in (1, 2, 3):
                arrived(got3.at[t, p, o - 1], r3.at[t, p, o - 1], s3.at[0, 0, 0])
            mine = part3[t, p, (zhi - zlo + 4) % 4]
            refout[t, :, PAIR * p : PAIR * (p + 1)] = total(mine, got3.at[t, p]) * (factor * (SCALE if t == 0 else 1.0))
    for t, a in enumerate((grk_out, grv_out)):
        out.append(pltpu.make_async_copy(refout.at[t], a, out_sem.at[3 + t]))
        out[-1].start()
    for copy in sent:
        copy.wait_send()
    for copy in out:
        copy.wait()


def per_device(queries, keys, values, out_grad, ref_keys, ref_values, frame_weight):
    hbm = pl.BlockSpec(memory_space=pl.ANY)
    shape = jax.ShapeDtypeStruct
    vmem, dma = pltpu.VMEM, pltpu.SemaphoreType.DMA
    return pl.pallas_call(
        kernel,
        name="joint_attention_grads",
        out_shape=(
            shape((SEQ, WIDTH), BF),
            shape((SEQ, WIDTH), BF),
            shape((SEQ, WIDTH), BF),
            shape((16, WIDTH), F32),
            shape((16, WIDTH), F32),
        ),
        in_specs=[hbm] * 6 + [pl.BlockSpec(memory_space=pltpu.SMEM)],
        out_specs=[hbm] * 5,
        scratch_shapes=[
            vmem((4, SEQ, WIDTH), BF),
            vmem((2, 2, 4, 2, 4, 32, PAIR), BF),
            vmem((2, 2, 2 * SEQ, PAIR), BF),
            vmem((2, 2, PAIR, 2 * SEQ), BF),
            vmem((2, 5, SEQ, 2 * SEQ), F32),
            vmem((2, 5, SEQ, 2 * SEQ), F32),
            vmem((2, 5, SEQ, 2 * SEQ), BF),
            vmem((2, PAIR, SEQ), F32),
            vmem((2, 2, SEQ, PAIR), F32),
            vmem((3, SEQ, WIDTH), BF),
            vmem((2, 2, 4, 4, 4, 16, PAIR), BF),
            vmem((2, 2, 3, 4, 4, 16, PAIR), BF),
            vmem((2, 2, 4, 4, 16, PAIR), BF),
            vmem((2, 2, 3, 4, 16, PAIR), BF),
            vmem((2, 2, 4, 16, PAIR), BF),
            vmem((2, 2, 3, 16, PAIR), BF),
            vmem((4, 8, 128), F32),
            vmem((3, 3, 8, 128), F32),
            vmem((2, 16, WIDTH), F32),
            dma((8,)),
            dma((5,)),
            dma((2, 2, 3, 2)),
            dma((2, 2)),
            dma((2, 2)),
            dma((2, 2)),
            dma((2, 2, 3)),
            dma((2, 2, 3)),
            dma((2, 2, 3)),
            dma((2, 2, 3)),
            dma((2, 2, 3)),
            dma((2, 2, 3)),
            dma((2, 2, 3)),
            dma((2, 2, 3)),
            dma((3, 3)),
            dma((3, 3)),
        ],
        compiler_params=pltpu.CompilerParams(
            collective_id=0, has_side_effects=True, vmem_limit_bytes=44 * 2**20
        ),
    )(
        queries,
        keys,
        values,
        out_grad,
        ref_keys.reshape(4, 32, -1),
        ref_values.reshape(4, 32, -1),
        frame_weight,
    )


def solution(mesh):
    tokens = P("frame", "ref")
    return jax.shard_map(
        per_device,
        mesh=mesh,
        in_specs=(tokens, tokens, tokens, tokens, P("ref", None), P("ref", None), P("frame")),
        out_specs=(tokens,) * 5,
        check_vma=False,
    )
```

```python
import jax
import jax.numpy as jnp
from jax import lax
from jax.experimental import pallas as pl
from jax.experimental.pallas import tpu as pltpu
from jax.sharding import PartitionSpec as P

F32, BF = jnp.float32, jnp.bfloat16
MESH = pl.DeviceIdType.MESH
SCALE = 0.125
EXP2_SCALE = SCALE * 1.4426950408889634
SEQ, WIDTH, PAIR = 256, 256, 128
FRAMES = 64
KEY, VALUE = 0, 1


def dot(a, b):
    return lax.dot_general(a, b, (((1,), (0,)), ((), ())), preferred_element_type=F32)


def fold(a):
    return jnp.sum(a.reshape(-1, 8, a.shape[-1]), axis=0)


def split_heads(p, a, stacked, across):
    a = a[:, PAIR * p : PAIR * (p + 1)]
    low = lax.broadcasted_iota(jnp.int32, (SEQ, PAIR), 1) < 64
    zero = jnp.zeros((SEQ, PAIR), BF)
    stacked[p, 0:SEQ] = jnp.where(low, a, zero)
    stacked[p, SEQ:] = jnp.where(low, zero, a)
    turned = a.T
    top = lax.broadcasted_iota(jnp.int32, (PAIR, SEQ), 0) < 64
    zero = jnp.zeros((PAIR, SEQ), BF)
    across[p, :, 0:SEQ] = jnp.where(top, turned, zero)
    across[p, :, SEQ:] = jnp.where(top, zero, turned)


def kernel(
    q_in, k_in, v_in, d_in, rk_in, rv_in, w_in,
    gq_out, gk_out, gv_out, grk_out, grv_out,
    own, refs, stacked, across, raised, gshare, gscore, gq_t, gkv, result,
    part, got1, part2, got2, part3, got3, own_weight, weights, weights_got, refout,
    loc_sem, out_sem, zs, zr, cs, cr, gs, gr, s1, r1, s2, r2, s3, r3, ws, wr, hop_sem,
):
    frame, ref = lax.axis_index("frame"), lax.axis_index("ref")
    zhi, x, y = frame // 16, (frame // 4) % 4, frame % 4
    zlo, core = ref // 2, ref % 2

    def at(dx=0, dy=0, dz=0, c=core):
        z = (zhi * 4 + zlo + dz + 16) % 16
        return (((z // 4) * 4 + (x + dx) % 4) * 4 + (y + dy) % 4, (z % 4) * 2 + c)

    def signal(sem, device):
        pl.semaphore_signal(sem, inc=1, device_id=device, device_id_type=MESH)

    near = [at(c=1 - core)]
    near += [at(dz=dz, c=c) for dz in (1, -1, 2, -2) for c in (0, 1)]
    near += [at(dx=o) for o in (1, 2, 3)] + [at(dy=o) for o in (1, 2, 3)]
    barrier = pltpu.get_barrier_semaphore()
    for device in near:
        signal(barrier, device)

    def columns(r, h):
        return pl.ds(pl.multiple_of(r * WIDTH + h * PAIR, PAIR), PAIR)

    ref_in = (rk_in, rv_in)
    local = [pltpu.make_async_copy(a, own.at[i], loc_sem.at[i]) for i, a in enumerate((q_in, d_in, k_in, v_in))]
    local_ref = [
        [pltpu.make_async_copy(ref_in[t].at[:, :, columns(ref, h)], refs.at[t, h, 0, core], loc_sem.at[4 + 2 * h + t]) for t in (0, 1)]
        for h in (0, 1)
    ]
    weight_copy = pltpu.make_async_copy(w_in, own_weight, loc_sem.at[8])
    for copy in [weight_copy] + local + local_ref[0] + local_ref[1]:
        copy.start()
    pl.semaphore_wait(barrier, len(near))
    for dz in (2, -2):
        signal(hop_sem.at[0], at(dz=dz))

    sent = []

    def send(src, dst, send_sem, recv_sem, device):
        copy = pltpu.make_async_remote_copy(src, dst, send_sem, recv_sem, device_id=device, device_id_type=MESH)
        copy.start()
        sent.append(copy)

    def arrived(region, sem, any_send_sem):
        pltpu.make_async_remote_copy(region, region, any_send_sem, sem, device_id=at(dx=1), device_id_type=MESH).wait_recv()

    quarter = (x, y)
    groups = ((1, 3), (3, 4))
    for h in (0, 1):
        for group, hops in enumerate((((1, 2), (-1, 1)), ((2, 3),))):
            for t in (0, 1):
                for dz, place in hops:
                    for c in (0, 1):
                        target = at(dz=-dz if place == 3 and t == 1 else dz, c=c)
                        here = ref_in[t].at[quarter[t], :, columns(target[1], h)]
                        send(here, refs.at[t, h, place, core, quarter[t]], zs.at[h, t, place - 1, c], zr.at[h, t, group], target)
    weight_copy.wait()
    weights[0] = jnp.broadcast_to(own_weight[...], (8, 128))
    for h in (0, 1):
        for t in (0, 1):
            here = ref_in[t].at[:, :, columns(zlo * 2 + 1 - core, h)]
            send(here, refs.at[t, h, 0, core], cs.at[h, t], cr.at[h, t], at(c=1 - core))
    for o in (1, 2, 3):
        send(weights.at[0], weights_got.at[0, o - 1], ws.at[0, o - 1], wr.at[0, o - 1], at(dx=o))

    def gather_planes(h, group):
        first, last = groups[group]
        for t in (0, 1):
            mine = refs.at[t, h, first:last, :, quarter[t]]
            arrived(mine, zr.at[h, t, group], zs.at[0, 0, 0, 0])
            for o in (1, 2, 3):
                send(mine, mine, gs.at[h, t, group, o - 1], gr.at[h, t, group, o - 1], at(dx=o) if t == 0 else at(dy=o))

    def wait_planes(h, group):
        first, last = groups[group]
        for t in (0, 1):
            for o in (1, 2, 3):
                arrived(refs.at[t, h, first:last, :, (quarter[t] + 4 - o) % 4], gr.at[h, t, group, o - 1], gs.at[0, 0, 0, 0])

    totals = [None, None]

    def scores(p, j, keys, values):
        e = jnp.exp2(dot(keys, across[0, p]) * EXP2_SCALE)
        g = dot(values, across[1, p])
        raised[p, j] = e
        gshare[p, j] = g
        more = (fold(e), fold(e * g))
        totals[p] = more if totals[p] is None else (totals[p][0] + more[0], totals[p][1] + more[1])

    def ref_chunk(t, p, s):
        return refs[t, p, s].reshape(SEQ, PAIR)

    def ref_scores(p, s):
        scores(p, s, ref_chunk(0, p, s), ref_chunk(1, p, s))

    def own_chunk(i, p):
        return own[i, :, PAIR * p : PAIR * (p + 1)]

    def weight_stage(stage):
        for o in (1, 2, 3):
            arrived(weights_got.at[stage, o - 1], wr.at[stage, o - 1], ws.at[0, 0])
        weights[stage + 1] = weights[stage] + weights_got[stage, 0] + weights_got[stage, 1] + weights_got[stage, 2]
        if stage < 2:
            for o in (1, 2, 3):
                target = at(dy=o) if stage == 0 else at(dz=4 * o)
                send(weights.at[stage + 1], weights_got.at[stage + 1, o - 1], ws.at[stage + 1, o - 1], wr.at[stage + 1, o - 1], target)

    local[0].wait()
    local[1].wait()
    for p in (0, 1):
        split_heads(p, own[0], stacked.at[0], across.at[0])
        split_heads(p, own[1], stacked.at[1], across.at[1])
    gather_planes(0, 0)
    local[2].wait()
    local[3].wait()
    scores(0, 4, own_chunk(2, 0), own_chunk(3, 0))
    gather_planes(0, 1)
    scores(1, 4, own_chunk(2, 1), own_chunk(3, 1))
    gather_planes(1, 0)
    gather_planes(1, 1)
    pl.semaphore_wait(hop_sem.at[0], 2)
    for dz in (4, -4):
        signal(hop_sem.at[1], at(dz=dz))
    weight_stage(0)
    for h in (0, 1):
        for t in (0, 1):
            local_ref[h][t].wait()
            arrived(refs.at[t, h, 0, 1 - core], cr.at[h, t], cs.at[0, 0])
        ref_scores(h, 0)

    def shares(p, j, norm):
        share = raised[p, j] * norm[0]
        score = (share * (gshare[p, j] - norm[1])).astype(BF)
        gscore[p, j] = score
        return dot(score, stacked[0, p]), dot(share.astype(BF), stacked[1, p])

    norms = [None, None]

    def normalise(p):
        norm = 1.0 / jnp.sum(totals[p][0], axis=0, keepdims=True)
        norms[p] = (norm, jnp.sum(totals[p][1], axis=0, keepdims=True) * norm)

    order = (2, 1, 3, 0)
    parts = ((0, 1), (1, 4))
    weight = own_weight[...]

    def first_stage(p, group):
        first, last = parts[group]
        for i in range(first, last):
            step = (zhi + order[i] - zlo + 4) % 4
            place = step + (step // 2) * (5 - 2 * step)
            for t, grad in enumerate(shares(p, place, norms[p])):
                part[t, p, i] = (grad * weight).astype(BF).reshape(4, 4, 16, PAIR)
        for o in (1, 2, 3):
            for t in (0, 1):
                here = part.at[0, p, first:last, (x + o) % 4] if t == 0 else part.at[1, p, first:last, :, (y + o) % 4]
                send(here, got1.at[t, p, o - 1, first:last], s1.at[t, p, group, o - 1], r1.at[t, p, group, o - 1], at(dx=o) if t == 0 else at(dy=o))

    def total(first, got):
        return first.astype(F32) + got[0].astype(F32) + got[1].astype(F32) + got[2].astype(F32)

    def second_stage(p, group):
        first, last = parts[group]
        for t in (0, 1):
            for o in (1, 2, 3):
                arrived(got1.at[t, p, o - 1, first:last], r1.at[t, p, group, o - 1], s1.at[0, 0, 0, 0])
            mine = part[0, p, first:last, x] if t == 0 else part[1, p, first:last, :, y]
            part2[t, p, first:last] = total(mine, got1[t, p, :, first:last]).astype(BF)
            for o in (1, 2, 3):
                here = part2.at[t, p, first:last, (y + o) % 4 if t == 0 else (x + o) % 4]
                send(here, got2.at[t, p, o - 1, first:last], s2.at[t, p, group, o - 1], r2.at[t, p, group, o - 1], at(dy=o) if t == 0 else at(dx=o))

    def third_stage(p, group):
        first, last = parts[group]
        for t in (0, 1):
            for o in (1, 2, 3):
                arrived(got2.at[t, p, o - 1, first:last], r2.at[t, p, group, o - 1], s2.at[0, 0, 0, 0])
            part3[p, first:last, t] = total(part2[t, p, first:last, y if t == 0 else x], got2[t, p, :, first:last]).astype(BF)
        for i in range(first, min(last, 3)):
            send(part3.at[p, i], got3.at[p, i], s3.at[p, i], r3.at[p, i], at(dz=4 * order[i]))

    def frame_grads(p):
        gk, gv = shares(p, 4, norms[p])
        gkv[0, p] = gk
        gkv[1, p] = gv
        sums = [None, None]
        for j in range(5):
            turned = (own_chunk(2, p) if j == 4 else ref_chunk(0, p, j)).T
            for a in (0, 1):
                more = dot(turned[64 * a : 64 * (a + 1)], gscore[p, j, :, SEQ * a : SEQ * (a + 1)])
                sums[a] = more if sums[a] is None else sums[a] + more
        gq_t[p, 0:64] = sums[0]
        gq_t[p, 64:128] = sums[1]

    wait_planes(0, 0)
    ref_scores(0, 1)
    ref_scores(0, 2)
    wait_planes(0, 1)
    ref_scores(0, 3)
    normalise(0)
    first_stage(0, 0)
    first_stage(0, 1)
    pl.semaphore_wait(hop_sem.at[1], 2)
    weight_stage(1)
    wait_planes(1, 0)
    ref_scores(1, 1)
    ref_scores(1, 2)
    wait_planes(1, 1)
    ref_scores(1, 3)
    normalise(1)
    first_stage(1, 0)
    first_stage(1, 1)
    second_stage(0, 0)
    second_stage(0, 1)
    second_stage(1, 0)
    third_stage(0, 0)
    third_stage(0, 1)
    second_stage(1, 1)
    third_stage(1, 0)
    third_stage(1, 1)
    frame_grads(0)
    frame_grads(1)
    weight_stage(2)
    factor = FRAMES / weights[3, 0:1, 0:1]
    own_factor = weight * factor
    for p in (0, 1):
        cols = slice(PAIR * p, PAIR * (p + 1))
        result[0, :, cols] = (gq_t[p].T * (own_factor * SCALE)).astype(BF)
        result[1, :, cols] = (gkv[0, p] * (own_factor * SCALE)).astype(BF)
        result[2, :, cols] = (gkv[1, p] * own_factor).astype(BF)
    out = [pltpu.make_async_copy(result.at[i], a, out_sem.at[i]) for i, a in enumerate((gq_out, gk_out, gv_out))]
    for copy in out:
        copy.start()
    for copy in sent:
        copy.wait_send()
    for p in (0, 1):
        for i in range(3):
            arrived(got3.at[p, i], r3.at[p, i], s3.at[0, 0])
        sums = total(part3[p, 3], got3[p])
        for t in (0, 1):
            refout[t, :, PAIR * p : PAIR * (p + 1)] = sums[t] * (factor * (SCALE if t == 0 else 1.0))
    for t, a in enumerate((grk_out, grv_out)):
        out.append(pltpu.make_async_copy(refout.at[t], a, out_sem.at[3 + t]))
        out[-1].start()
    for copy in out:
        copy.wait()


def hand_on(*refs):
    ins, outs, held, sem_in, sem_out = refs[0:5], refs[5:10], refs[10:15], refs[15], refs[16]
    into = [pltpu.make_async_copy(ins[i], held[i], sem_in.at[i]) for i in range(5)]
    out = [pltpu.make_async_copy(held[i], outs[i], sem_out.at[i]) for i in range(5)]
    for copy in into:
        copy.start()
    for i in range(5):
        into[i].wait()
        out[i].start()
    for copy in out:
        copy.wait()


def per_device(queries, keys, values, out_grad, ref_keys, ref_values, frame_weight):
    hbm = pl.BlockSpec(memory_space=pl.ANY)
    shape = jax.ShapeDtypeStruct
    vmem, dma = pltpu.VMEM, pltpu.SemaphoreType.DMA
    out_shape = (shape((SEQ, WIDTH), BF),) * 3 + (shape((16, WIDTH), F32),) * 2
    grads = pl.pallas_call(
        kernel,
        name="joint_attention_grads",
        out_shape=out_shape,
        in_specs=[hbm] * 7,
        out_specs=[hbm] * 5,
        scratch_shapes=[
            vmem((4, SEQ, WIDTH), BF),
            vmem((2, 2, 4, 2, 4, 32, PAIR), BF),
            vmem((2, 2, 2 * SEQ, PAIR), BF),
            vmem((2, 2, PAIR, 2 * SEQ), BF),
            vmem((2, 5, SEQ, 2 * SEQ), F32),
            vmem((2, 5, SEQ, 2 * SEQ), F32),
            vmem((2, 5, SEQ, 2 * SEQ), BF),
            vmem((2, PAIR, SEQ), F32),
            vmem((2, 2, SEQ, PAIR), F32),
            vmem((3, SEQ, WIDTH), BF),
            vmem((2, 2, 4, 4, 4, 16, PAIR), BF),
            vmem((2, 2, 3, 4, 4, 16, PAIR), BF),
            vmem((2, 2, 4, 4, 16, PAIR), BF),
            vmem((2, 2, 3, 4, 16, PAIR), BF),
            vmem((2, 4, 2, 16, PAIR), BF),
            vmem((2, 3, 2, 16, PAIR), BF),
            vmem((1, 1), F32),
            vmem((4, 8, 128), F32),
            vmem((3, 3, 8, 128), F32),
            vmem((2, 16, WIDTH), F32),
            dma((9,)),
            dma((5,)),
            dma((2, 2, 3, 2)),
            dma((2, 2, 2)),
            dma((2, 2)),
            dma((2, 2)),
            dma((2, 2, 2, 3)),
            dma((2, 2, 2, 3)),
            dma((2, 2, 2, 3)),
            dma((2, 2, 2, 3)),
            dma((2, 2, 2, 3)),
            dma((2, 2, 2, 3)),
            dma((2, 3)),
            dma((2, 3)),
            dma((3, 3)),
            dma((3, 3)),
            pltpu.SemaphoreType.REGULAR((2,)),
        ],
        compiler_params=pltpu.CompilerParams(collective_id=0, has_side_effects=True, vmem_limit_bytes=62 * 2**20),
    )(
        queries,
        keys,
        values,
        out_grad,
        ref_keys.reshape(4, 32, -1),
        ref_values.reshape(4, 32, -1),
        frame_weight.reshape(1, 1),
    )
    return pl.pallas_call(
        hand_on,
        name="hand_on",
        out_shape=out_shape,
        in_specs=[hbm] * 5,
        out_specs=[hbm] * 5,
        scratch_shapes=[vmem(a.shape, a.dtype) for a in out_shape] + [dma((5,)), dma((5,))],
    )(*grads)


def solution(mesh):
    tokens = P("frame", "ref")
    return jax.shard_map(
        per_device,
        mesh=mesh,
        in_specs=(tokens, tokens, tokens, tokens, P("ref", None), P("ref", None), P("frame")),
        out_specs=(tokens,) * 5,
        check_vma=False,
    )
```

```python
import jax
import jax.numpy as jnp
from jax import lax
from jax.experimental import pallas as pl
from jax.experimental.pallas import tpu as pltpu
from jax.sharding import PartitionSpec as P

F32, BF = jnp.float32, jnp.bfloat16
MESH = pl.DeviceIdType.MESH
SCALE = 0.125
EXP2_SCALE = SCALE * 1.4426950408889634
SEQ, WIDTH, PAIR = 256, 256, 128
FRAMES = 64
KEY, VALUE = 0, 1


def dot(a, b):
    return lax.dot_general(a, b, (((1,), (0,)), ((), ())), preferred_element_type=F32)


def fold(a):
    return jnp.sum(a.reshape(-1, 8, a.shape[-1]), axis=0)


def split_heads(p, a, stacked, across):
    a = a[:, PAIR * p : PAIR * (p + 1)]
    low = lax.broadcasted_iota(jnp.int32, (SEQ, PAIR), 1) < 64
    zero = jnp.zeros((SEQ, PAIR), BF)
    stacked[p, 0:SEQ] = jnp.where(low, a, zero)
    stacked[p, SEQ:] = jnp.where(low, zero, a)
    turned = a.T
    top = lax.broadcasted_iota(jnp.int32, (PAIR, SEQ), 0) < 64
    zero = jnp.zeros((PAIR, SEQ), BF)
    across[p, :, 0:SEQ] = jnp.where(top, turned, zero)
    across[p, :, SEQ:] = jnp.where(top, zero, turned)


def kernel(
    q_in, k_in, v_in, d_in, rk_in, rv_in, w_in,
    gq_out, gk_out, gv_out, grk_out, grv_out,
    own, refs, stacked, across, raised, gshare, gscore, gq_t, gkv,
    part, got1, part2, got2, part3, got3, own_weight, weights, weights_got,
    loc_sem, sent_sem, zr, cr, gr, r1, r2, r3, wr, hop_sem,
):
    frame, ref = lax.axis_index("frame"), lax.axis_index("ref")
    zhi, x, y = frame // 16, (frame // 4) % 4, frame % 4
    zlo, core = ref // 2, ref % 2

    def at(dx=0, dy=0, dz=0, c=core):
        z = (zhi * 4 + zlo + dz + 16) % 16
        return (((z // 4) * 4 + (x + dx) % 4) * 4 + (y + dy) % 4, (z % 4) * 2 + c)

    def signal(sem, device):
        pl.semaphore_signal(sem, inc=1, device_id=device, device_id_type=MESH)

    near = [at(c=1 - core)]
    near += [at(dz=dz, c=c) for dz in (1, -1, 2, -2) for c in (0, 1)]
    near += [at(dx=o) for o in (1, 2, 3)] + [at(dy=o) for o in (1, 2, 3)]
    barrier = pltpu.get_barrier_semaphore()
    for device in near:
        signal(barrier, device)

    def columns(r, h):
        return pl.ds(pl.multiple_of(r * WIDTH + h * PAIR, PAIR), PAIR)

    ref_in = (rk_in, rv_in)
    weight_copy = pltpu.make_async_copy(w_in, own_weight, loc_sem.at[0])
    weight_copy.start()
    for i, a in enumerate((q_in, d_in, k_in, v_in)):
        pltpu.make_async_copy(a, own.at[i], loc_sem.at[1 + i // 2]).start()
    for h in (0, 1):
        for t in (0, 1):
            pltpu.make_async_copy(ref_in[t].at[:, :, columns(ref, h)], refs.at[t, h, 0, core], loc_sem.at[3 + h]).start()

    def copied(region, sem):
        pltpu.make_async_copy(region, region, sem).wait()

    pl.semaphore_wait(barrier, len(near))
    for dz in (2, -2):
        signal(hop_sem.at[0], at(dz=dz))

    def send(src, dst, phase, recv_sem, device):
        pltpu.make_async_remote_copy(src, dst, sent_sem.at[phase], recv_sem, device_id=device, device_id_type=MESH).start()

    def arrived(region, sem):
        pltpu.make_async_remote_copy(region, region, sent_sem.at[0], sem, device_id=at(dx=1), device_id_type=MESH).wait_recv()

    def all_sent(region, phase):
        pltpu.make_async_remote_copy(region, region, sent_sem.at[phase], wr.at[0], device_id=at(dx=1), device_id_type=MESH).wait_send()

    quarter = (x, y)
    groups = ((1, 3), (3, 4))
    for h, group, hops in ((0, 1, ((2, 3),)), (1, 0, ((1, 2), (-1, 1))), (1, 1, ((2, 3),))):
        for t in (0, 1):
            for dz, place in hops:
                for c in (0, 1):
                    target = at(dz=-dz if place == 3 and t == 1 else dz, c=c)
                    here = ref_in[t].at[quarter[t], :, columns(target[1], h)]
                    send(here, refs.at[t, h, place, core, quarter[t]], 0, zr.at[h, t, group], target)
    for t in (0, 1):
        for dz, place in ((1, 2), (-1, 1)):
            for c in (0, 1):
                target = at(dz=dz, c=c)
                send(ref_in[t].at[:, :, columns(target[1], 0)], refs.at[t, 0, place, core], 0, gr.at[0, 0], target)
    weight_copy.wait()
    weight = own_weight[0]
    weights[0] = jnp.full((8, 128), weight, F32)
    for h in (0, 1):
        for t in (0, 1):
            here = ref_in[t].at[:, :, columns(zlo * 2 + 1 - core, h)]
            send(here, refs.at[t, h, 0, core], 0, cr.at[h], at(c=1 - core))
    for o in (1, 2, 3):
        send(weights.at[0], weights_got.at[0, o - 1], 2, wr.at[0], at(dx=o))

    def gather_planes(h, group):
        first, last = groups[group]
        for t in (0, 1):
            mine = refs.at[t, h, first:last, :, quarter[t]]
            arrived(mine, zr.at[h, t, group])
            for o in (1, 2, 3):
                send(mine, mine, 0, gr.at[h, group], at(dx=o) if t == 0 else at(dy=o))

    def wait_planes(h, group):
        first, last = groups[group]
        arrived(refs.at[:, h, first:last] if (h, group) == (0, 0) else refs.at[:, h, first:last, :, 0:3], gr.at[h, group])

    totals = [None, None]

    def scores(p, j, keys, values):
        e = jnp.exp2(dot(keys, across[0, p]) * EXP2_SCALE)
        g = dot(values, across[1, p])
        raised[p, j] = e
        gshare[p, j] = g
        more = (fold(e), fold(e * g))
        totals[p] = more if totals[p] is None else (totals[p][0] + more[0], totals[p][1] + more[1])

    def ref_chunk(t, p, s):
        return refs[t, p, s].reshape(SEQ, PAIR)

    def ref_scores(p, s):
        scores(p, s, ref_chunk(0, p, s), ref_chunk(1, p, s))

    def own_chunk(i, p):
        return own[i, :, PAIR * p : PAIR * (p + 1)]

    def weight_stage(stage):
        arrived(weights_got.at[stage], wr.at[stage])
        weights[stage + 1] = weights[stage] + weights_got[stage, 0] + weights_got[stage, 1] + weights_got[stage, 2]
        if stage < 2:
            for o in (1, 2, 3):
                target = at(dy=o) if stage == 0 else at(dz=4 * o)
                send(weights.at[stage + 1], weights_got.at[stage + 1, o - 1], 2, wr.at[stage + 1], target)

    copied(own.at[0:2], loc_sem.at[1])
    for p in (0, 1):
        split_heads(p, own[0], stacked.at[0], across.at[0])
        split_heads(p, own[1], stacked.at[1], across.at[1])
    copied(own.at[2:4], loc_sem.at[2])
    scores(0, 4, own_chunk(2, 0), own_chunk(3, 0))
    gather_planes(0, 1)
    gather_planes(1, 0)
    scores(1, 4, own_chunk(2, 1), own_chunk(3, 1))
    gather_planes(1, 1)
    pl.semaphore_wait(hop_sem.at[0], 2)
    for dz in (4, -4):
        signal(hop_sem.at[1], at(dz=dz))
    weight_stage(0)
    for h in (0, 1):
        copied(refs.at[:, h, 0, core], loc_sem.at[3 + h])
        arrived(refs.at[:, h, 0, 1 - core], cr.at[h])
        ref_scores(h, 0)

    def shares(p, j, norm):
        share = raised[p, j] * norm[0]
        score = (share * (gshare[p, j] - norm[1])).astype(BF)
        gscore[p, j] = score
        return dot(score, stacked[0, p]), dot(share.astype(BF), stacked[1, p])

    norms = [None, None]

    def normalise(p):
        norm = 1.0 / jnp.sum(totals[p][0], axis=0, keepdims=True)
        norms[p] = (norm, jnp.sum(totals[p][1], axis=0, keepdims=True) * norm)

    order = (2, 1, 3, 0)
    parts = (((0, 3), (3, 4)), ((0, 1), (1, 3), (3, 4)))

    def first_stage(p, group):
        first, last = parts[p][group]
        for i in range(first, last):
            step = (zhi + order[i] - zlo + 4) % 4
            place = step + (step // 2) * (5 - 2 * step)
            for t, grad in enumerate(shares(p, place, norms[p])):
                part[t, p, i] = (grad * weight).astype(BF).reshape(4, 4, 16, PAIR)

    def first_send(p, group):
        first, last = parts[p][group]
        for o in (2, 1, 3):
            for t in (0, 1):
                here = part.at[0, p, first:last, (x + o) % 4] if t == 0 else part.at[1, p, first:last, :, (y + o) % 4]
                send(here, got1.at[t, p, o - 1, first:last], 1, r1.at[p, group], at(dx=o) if t == 0 else at(dy=o))

    def total(first, got):
        return first.astype(F32) + got[0].astype(F32) + got[1].astype(F32) + got[2].astype(F32)

    def second_stage(p, group):
        first, last = parts[p][group]
        arrived(got1.at[:, p, :, first:last], r1.at[p, group])
        for t in (0, 1):
            mine = part[0, p, first:last, x] if t == 0 else part[1, p, first:last, :, y]
            part2[t, p, first:last] = total(mine, got1[t, p, :, first:last]).astype(BF)
            for o in (2, 1, 3):
                here = part2.at[t, p, first:last, (y + o) % 4 if t == 0 else (x + o) % 4]
                send(here, got2.at[t, p, o - 1, first:last], 1, r2.at[p, group], at(dy=o) if t == 0 else at(dx=o))

    def third_stage(p, group):
        first, last = parts[p][group]
        arrived(got2.at[:, p, :, first:last], r2.at[p, group])
        for t in (0, 1):
            part3[p, first:last, t] = total(part2[t, p, first:last, y if t == 0 else x], got2[t, p, :, first:last]).astype(BF)
        for i in range(first, min(last, 3)):
            send(part3.at[p, i], got3.at[p, i], 1, r3.at[p], at(dz=4 * order[i]))

    def frame_grads(p):
        gk, gv = shares(p, 4, norms[p])
        gkv[0, p] = gk
        gkv[1, p] = gv
        sums = [None, None]
        for j in range(5):
            turned = (own_chunk(2, p) if j == 4 else ref_chunk(0, p, j)).T
            for a in (0, 1):
                more = dot(turned[64 * a : 64 * (a + 1)], gscore[p, j, :, SEQ * a : SEQ * (a + 1)])
                sums[a] = more if sums[a] is None else sums[a] + more
        gq_t[p, 0:64] = sums[0]
        gq_t[p, 64:128] = sums[1]

    wait_planes(0, 0)
    ref_scores(0, 1)
    ref_scores(0, 2)
    wait_planes(0, 1)
    ref_scores(0, 3)
    normalise(0)
    first_stage(0, 0)
    first_send(0, 0)
    first_stage(0, 1)
    wait_planes(1, 0)
    ref_scores(1, 1)
    ref_scores(1, 2)
    wait_planes(1, 1)
    ref_scores(1, 3)
    normalise(1)
    first_stage(1, 0)
    first_send(1, 0)
    first_stage(1, 1)
    first_send(1, 1)
    first_send(0, 1)
    first_stage(1, 2)
    first_send(1, 2)
    pl.semaphore_wait(hop_sem.at[1], 2)
    weight_stage(1)
    second_stage(0, 0)
    second_stage(1, 0)
    second_stage(1, 1)
    third_stage(0, 0)
    third_stage(1, 0)
    second_stage(0, 1)
    second_stage(1, 2)
    third_stage(1, 1)
    frame_grads(0)
    frame_grads(1)
    third_stage(0, 1)
    third_stage(1, 2)
    weight_stage(2)
    factor = FRAMES / weights[3, 0:1, 0:1]
    own_factor = weight * factor
    for p in (0, 1):
        cols = slice(PAIR * p, PAIR * (p + 1))
        gq_out[:, cols] = (gq_t[p].T * (own_factor * SCALE)).astype(BF)
        gk_out[:, cols] = (gkv[0, p] * (own_factor * SCALE)).astype(BF)
        gv_out[:, cols] = (gkv[1, p] * own_factor).astype(BF)
    all_sent(raised.at[0, 0:2, 0:224], 0)
    all_sent(raised.at[0, 0:3, 0:168], 1)
    all_sent(weights_got, 2)
    for p in (0, 1):
        arrived(got3.at[p], r3.at[p])
        sums = total(part3[p, 3], got3[p])
        grk_out[:, PAIR * p : PAIR * (p + 1)] = sums[0] * (factor * SCALE)
        grv_out[:, PAIR * p : PAIR * (p + 1)] = sums[1] * factor


def hand_on(*refs):
    copies = [pltpu.make_async_copy(refs[i], refs[5 + i], refs[10].at[i]) for i in range(5)]
    for copy in copies:
        copy.start()
    for copy in copies:
        copy.wait()


def per_device(queries, keys, values, out_grad, ref_keys, ref_values, frame_weight):
    hbm = pl.BlockSpec(memory_space=pl.ANY)
    shape = jax.ShapeDtypeStruct
    vmem, dma = pltpu.VMEM, pltpu.SemaphoreType.DMA
    out_shape = (shape((SEQ, WIDTH), BF),) * 3 + (shape((16, WIDTH), F32),) * 2
    grads = pl.pallas_call(
        kernel,
        name="joint_attention_grads",
        out_shape=tuple(pltpu.VMEM(a.shape, a.dtype) for a in out_shape),
        in_specs=[hbm] * 7,
        out_specs=[pl.BlockSpec(memory_space=pltpu.VMEM)] * 5,
        scratch_shapes=[
            vmem((4, SEQ, WIDTH), BF),
            vmem((2, 2, 4, 2, 4, 32, PAIR), BF),
            vmem((2, 2, 2 * SEQ, PAIR), BF),
            vmem((2, 2, PAIR, 2 * SEQ), BF),
            vmem((2, 5, SEQ, 2 * SEQ), F32),
            vmem((2, 5, SEQ, 2 * SEQ), F32),
            vmem((2, 5, SEQ, 2 * SEQ), BF),
            vmem((2, PAIR, SEQ), F32),
            vmem((2, 2, SEQ, PAIR), F32),
            vmem((2, 2, 4, 4, 4, 16, PAIR), BF),
            vmem((2, 2, 3, 4, 4, 16, PAIR), BF),
            vmem((2, 2, 4, 4, 16, PAIR), BF),
            vmem((2, 2, 3, 4, 16, PAIR), BF),
            vmem((2, 4, 2, 16, PAIR), BF),
            vmem((2, 3, 2, 16, PAIR), BF),
            pltpu.SMEM((1,), F32),
            vmem((4, 8, 128), F32),
            vmem((3, 3, 8, 128), F32),
            dma((5,)),
            dma((3,)),
            dma((2, 2, 2)),
            dma((2,)),
            dma((2, 2)),
            dma((2, 3)),
            dma((2, 3)),
            dma((2,)),
            dma((3,)),
            pltpu.SemaphoreType.REGULAR((2,)),
        ],
        compiler_params=pltpu.CompilerParams(collective_id=0, has_side_effects=True, vmem_limit_bytes=62 * 2**20),
    )(
        queries,
        keys,
        values,
        out_grad,
        ref_keys.reshape(4, 32, -1),
        ref_values.reshape(4, 32, -1),
        frame_weight,
    )
    return pl.pallas_call(
        hand_on,
        name="hand_on",
        out_shape=out_shape,
        in_specs=[pl.BlockSpec(memory_space=pltpu.VMEM)] * 5,
        out_specs=[hbm] * 5,
        scratch_shapes=[dma((5,))],
        compiler_params=pltpu.CompilerParams(vmem_limit_bytes=2**20),
    )(*grads)


def solution(mesh):
    tokens = P("frame", "ref")
    return jax.shard_map(
        per_device,
        mesh=mesh,
        in_specs=(tokens, tokens, tokens, tokens, P("ref", None), P("ref", None), P("frame")),
        out_specs=(tokens,) * 5,
        check_vma=False,
    )
```

```python
import jax
import jax.numpy as jnp
from jax import lax
from jax.experimental import pallas as pl
from jax.experimental.pallas import tpu as pltpu
from jax.sharding import PartitionSpec as P

F32, BF = jnp.float32, jnp.bfloat16
MESH = pl.DeviceIdType.MESH
SCALE = 0.125
EXP2_SCALE = SCALE * 1.4426950408889634
SEQ, WIDTH, PAIR = 256, 256, 128
FRAMES = 64
KEY, VALUE = 0, 1


def dot(a, b):
    return lax.dot_general(a, b, (((1,), (0,)), ((), ())), preferred_element_type=F32)


def fold(a):
    return jnp.sum(a.reshape(-1, 8, a.shape[-1]), axis=0)


def split_heads(p, a, stacked, across):
    a = a[:, PAIR * p : PAIR * (p + 1)]
    low = lax.broadcasted_iota(jnp.int32, (SEQ, PAIR), 1) < 64
    zero = jnp.zeros((SEQ, PAIR), BF)
    stacked[p, 0:SEQ] = jnp.where(low, a, zero)
    stacked[p, SEQ:] = jnp.where(low, zero, a)
    turned = a.T
    top = lax.broadcasted_iota(jnp.int32, (PAIR, SEQ), 0) < 64
    zero = jnp.zeros((PAIR, SEQ), BF)
    across[p, :, 0:SEQ] = jnp.where(top, turned, zero)
    across[p, :, SEQ:] = jnp.where(top, zero, turned)


def kernel(
    q_in, k_in, v_in, d_in, rk_in, rv_in, w_in,
    gq_out, gk_out, gv_out, grk_out, grv_out,
    own, refs, stacked, across, raised, gshare, gscore, gq_t, gkv,
    part, got1, part2, got2, part3, got3, own_weight, weights, weights_got,
    loc_sem, sent_sem, zr, cr, gr, r1, r2, r3, wr, hop_sem,
):
    frame, ref = lax.axis_index("frame"), lax.axis_index("ref")
    zhi, x, y = frame // 16, (frame // 4) % 4, frame % 4
    zlo, core = ref // 2, ref % 2

    def at(dx=0, dy=0, dz=0, c=core):
        z = (zhi * 4 + zlo + dz + 16) % 16
        return (((z // 4) * 4 + (x + dx) % 4) * 4 + (y + dy) % 4, (z % 4) * 2 + c)

    def signal(sem, device):
        pl.semaphore_signal(sem, inc=1, device_id=device, device_id_type=MESH)

    near = [at(c=1 - core)]
    near += [at(dz=dz, c=c) for dz in (1, -1, 2, -2) for c in (0, 1)]
    near += [at(dx=o) for o in (1, 2, 3)] + [at(dy=o) for o in (1, 2, 3)]
    barrier = pltpu.get_barrier_semaphore()
    for device in near:
        signal(barrier, device)

    def columns(r, h):
        return pl.ds(pl.multiple_of(r * WIDTH + h * PAIR, PAIR), PAIR)

    ref_in = (rk_in, rv_in)
    weight_copy = pltpu.make_async_copy(w_in, own_weight, loc_sem.at[0])
    weight_copy.start()
    for i, a in enumerate((q_in, d_in, k_in, v_in)):
        pltpu.make_async_copy(a, own.at[i], loc_sem.at[1 + i // 2]).start()
    for h in (0, 1):
        for t in (0, 1):
            pltpu.make_async_copy(ref_in[t].at[:, :, columns(ref, h)], refs.at[t, h, 0, core], loc_sem.at[3 + h]).start()

    def copied(region, sem):
        pltpu.make_async_copy(region, region, sem).wait()

    pl.semaphore_wait(barrier, len(near))
    for dz in (2, -2):
        signal(hop_sem.at[0], at(dz=dz))

    def send(src, dst, phase, recv_sem, device):
        pltpu.make_async_remote_copy(src, dst, sent_sem.at[phase], recv_sem, device_id=device, device_id_type=MESH).start()

    def arrived(region, sem):
        pltpu.make_async_remote_copy(region, region, sent_sem.at[0], sem, device_id=at(dx=1), device_id_type=MESH).wait_recv()

    def all_sent(region, phase):
        pltpu.make_async_remote_copy(region, region, sent_sem.at[phase], wr.at[0], device_id=at(dx=1), device_id_type=MESH).wait_send()

    quarter = (x, y)
    for h in (0, 1):
        for t in (0, 1):
            for c in (0, 1):
                target = at(dz=2 if t == 0 else -2, c=c)
                here = ref_in[t].at[quarter[t], :, columns(target[1], h)]
                send(here, refs.at[t, h, 3, core, quarter[t]], 0, zr.at[h, t], target)
    for h in (0, 1):
        for t in (0, 1):
            for dz, place in ((1, 2), (-1, 1)):
                for c in (0, 1):
                    target = at(dz=dz, c=c)
                    send(ref_in[t].at[:, :, columns(target[1], h)], refs.at[t, h, place, core], 0, gr.at[h, 0], target)
    weight_copy.wait()
    weight = own_weight[0]
    weights[0] = jnp.full((8, 128), weight, F32)
    for h in (0, 1):
        for t in (0, 1):
            here = ref_in[t].at[:, :, columns(zlo * 2 + 1 - core, h)]
            send(here, refs.at[t, h, 0, core], 0, cr.at[h], at(c=1 - core))
    for o in (1, 2, 3):
        send(weights.at[0], weights_got.at[0, o - 1], 2, wr.at[0], at(dx=o))

    def gather_planes(h):
        for t in (0, 1):
            mine = refs.at[t, h, 3, :, quarter[t]]
            arrived(mine, zr.at[h, t])
            for o in (2, 1, 3):
                send(mine, mine, 0, gr.at[h, 1], at(dx=o) if t == 0 else at(dy=o))

    def wait_adjacent(h):
        arrived(refs.at[:, h, 1:3], gr.at[h, 0])

    def wait_planes(h):
        arrived(refs.at[:, h, 3, :, 0:3], gr.at[h, 1])

    totals = [None, None]

    def scores(p, j, keys, values):
        e = jnp.exp2(dot(keys, across[0, p]) * EXP2_SCALE)
        g = dot(values, across[1, p])
        raised[p, j] = e
        gshare[p, j] = g
        more = (fold(e), fold(e * g))
        totals[p] = more if totals[p] is None else (totals[p][0] + more[0], totals[p][1] + more[1])

    def ref_chunk(t, p, s):
        return refs[t, p, s].reshape(SEQ, PAIR)

    def ref_scores(p, s):
        scores(p, s, ref_chunk(0, p, s), ref_chunk(1, p, s))

    def own_chunk(i, p):
        return own[i, :, PAIR * p : PAIR * (p + 1)]

    def weight_stage(stage):
        arrived(weights_got.at[stage], wr.at[stage])
        weights[stage + 1] = weights[stage] + weights_got[stage, 0] + weights_got[stage, 1] + weights_got[stage, 2]
        if stage < 2:
            for o in (1, 2, 3):
                target = at(dy=o) if stage == 0 else at(dz=4 * o)
                send(weights.at[stage + 1], weights_got.at[stage + 1, o - 1], 2, wr.at[stage + 1], target)

    copied(own.at[0:2], loc_sem.at[1])
    for p in (0, 1):
        split_heads(p, own[0], stacked.at[0], across.at[0])
        split_heads(p, own[1], stacked.at[1], across.at[1])
    copied(own.at[2:4], loc_sem.at[2])
    scores(0, 4, own_chunk(2, 0), own_chunk(3, 0))
    scores(1, 4, own_chunk(2, 1), own_chunk(3, 1))
    gather_planes(0)
    gather_planes(1)
    pl.semaphore_wait(hop_sem.at[0], 2)
    for dz in (4, -4):
        signal(hop_sem.at[1], at(dz=dz))
    weight_stage(0)
    for h in (0, 1):
        copied(refs.at[:, h, 0, core], loc_sem.at[3 + h])
        arrived(refs.at[:, h, 0, 1 - core], cr.at[h])
        ref_scores(h, 0)

    def shares(p, j, norm):
        share = raised[p, j] * norm[0]
        score = (share * (gshare[p, j] - norm[1])).astype(BF)
        gscore[p, j] = score
        return dot(score, stacked[0, p]), dot(share.astype(BF), stacked[1, p])

    norms = [None, None]

    def normalise(p):
        norm = 1.0 / jnp.sum(totals[p][0], axis=0, keepdims=True)
        norms[p] = (norm, jnp.sum(totals[p][1], axis=0, keepdims=True) * norm)

    order = (2, 1, 3, 0)
    parts = (((0, 3), (3, 4)), ((0, 1), (1, 3), (3, 4)))

    def first_stage(p, group):
        first, last = parts[p][group]
        for i in range(first, last):
            step = (zhi + order[i] - zlo + 4) % 4
            place = step + (step // 2) * (5 - 2 * step)
            for t, grad in enumerate(shares(p, place, norms[p])):
                part[t, p, i] = (grad * weight).astype(BF).reshape(4, 4, 16, PAIR)

    def first_send(p, group):
        first, last = parts[p][group]
        for o in (2, 1, 3):
            for t in (0, 1):
                here = part.at[0, p, first:last, (x + o) % 4] if t == 0 else part.at[1, p, first:last, :, (y + o) % 4]
                send(here, got1.at[t, p, o - 1, first:last], 1, r1.at[p, group], at(dx=o) if t == 0 else at(dy=o))

    def total(first, got):
        return first.astype(F32) + got[0].astype(F32) + got[1].astype(F32) + got[2].astype(F32)

    def second_stage(p, group):
        first, last = parts[p][group]
        arrived(got1.at[:, p, :, first:last], r1.at[p, group])
        for t in (0, 1):
            mine = part[0, p, first:last, x] if t == 0 else part[1, p, first:last, :, y]
            part2[t, p, first:last] = total(mine, got1[t, p, :, first:last]).astype(BF)
            for o in (2, 1, 3):
                here = part2.at[t, p, first:last, (y + o) % 4 if t == 0 else (x + o) % 4]
                send(here, got2.at[t, p, o - 1, first:last], 1, r2.at[p, group], at(dy=o) if t == 0 else at(dx=o))

    def third_stage(p, group):
        first, last = parts[p][group]
        arrived(got2.at[:, p, :, first:last], r2.at[p, group])
        for t in (0, 1):
            part3[p, first:last, t] = total(part2[t, p, first:last, y if t == 0 else x], got2[t, p, :, first:last]).astype(BF)
        for i in range(first, min(last, 3)):
            send(part3.at[p, i], got3.at[p, i], 1, r3.at[p], at(dz=4 * order[i]))

    def frame_grads(p):
        gk, gv = shares(p, 4, norms[p])
        gkv[0, p] = gk
        gkv[1, p] = gv
        sums = [None, None]
        for j in range(5):
            turned = (own_chunk(2, p) if j == 4 else ref_chunk(0, p, j)).T
            for a in (0, 1):
                more = dot(turned[64 * a : 64 * (a + 1)], gscore[p, j, :, SEQ * a : SEQ * (a + 1)])
                sums[a] = more if sums[a] is None else sums[a] + more
        gq_t[p, 0:64] = sums[0]
        gq_t[p, 64:128] = sums[1]

    wait_adjacent(0)
    ref_scores(0, 1)
    ref_scores(0, 2)
    wait_planes(0)
    ref_scores(0, 3)
    normalise(0)
    first_stage(0, 0)
    first_send(0, 0)
    first_stage(0, 1)
    wait_planes(1)
    ref_scores(1, 3)
    wait_adjacent(1)
    ref_scores(1, 1)
    ref_scores(1, 2)
    normalise(1)
    first_stage(1, 0)
    first_send(1, 0)
    first_stage(1, 1)
    first_send(1, 1)
    first_send(0, 1)
    first_stage(1, 2)
    first_send(1, 2)
    pl.semaphore_wait(hop_sem.at[1], 2)
    weight_stage(1)
    second_stage(0, 0)
    second_stage(1, 0)
    second_stage(1, 1)
    third_stage(0, 0)
    third_stage(1, 0)
    second_stage(0, 1)
    second_stage(1, 2)
    third_stage(1, 1)
    frame_grads(0)
    frame_grads(1)
    third_stage(0, 1)
    third_stage(1, 2)
    weight_stage(2)
    factor = FRAMES / weights[3, 0:1, 0:1]
    own_factor = weight * factor
    for p in (0, 1):
        cols = slice(PAIR * p, PAIR * (p + 1))
        gq_out[:, cols] = (gq_t[p].T * (own_factor * SCALE)).astype(BF)
        gk_out[:, cols] = (gkv[0, p] * (own_factor * SCALE)).astype(BF)
        gv_out[:, cols] = (gkv[1, p] * own_factor).astype(BF)
    all_sent(raised.at[0, 0:2, 0:224], 0)
    all_sent(raised.at[0, 0:3, 0:168], 1)
    all_sent(weights_got, 2)
    for p in (0, 1):
        arrived(got3.at[p], r3.at[p])
        sums = total(part3[p, 3], got3[p])
        grk_out[:, PAIR * p : PAIR * (p + 1)] = sums[0] * (factor * SCALE)
        grv_out[:, PAIR * p : PAIR * (p + 1)] = sums[1] * factor


def hand_on(*refs):
    copies = [pltpu.make_async_copy(refs[i], refs[5 + i], refs[10].at[i]) for i in range(5)]
    for copy in copies:
        copy.start()
    for copy in copies:
        copy.wait()


def per_device(queries, keys, values, out_grad, ref_keys, ref_values, frame_weight):
    hbm = pl.BlockSpec(memory_space=pl.ANY)
    shape = jax.ShapeDtypeStruct
    vmem, dma = pltpu.VMEM, pltpu.SemaphoreType.DMA
    out_shape = (shape((SEQ, WIDTH), BF),) * 3 + (shape((16, WIDTH), F32),) * 2
    grads = pl.pallas_call(
        kernel,
        name="joint_attention_grads",
        out_shape=tuple(pltpu.VMEM(a.shape, a.dtype) for a in out_shape),
        in_specs=[hbm] * 7,
        out_specs=[pl.BlockSpec(memory_space=pltpu.VMEM)] * 5,
        scratch_shapes=[
            vmem((4, SEQ, WIDTH), BF),
            vmem((2, 2, 4, 2, 4, 32, PAIR), BF),
            vmem((2, 2, 2 * SEQ, PAIR), BF),
            vmem((2, 2, PAIR, 2 * SEQ), BF),
            vmem((2, 5, SEQ, 2 * SEQ), F32),
            vmem((2, 5, SEQ, 2 * SEQ), F32),
            vmem((2, 5, SEQ, 2 * SEQ), BF),
            vmem((2, PAIR, SEQ), F32),
            vmem((2, 2, SEQ, PAIR), F32),
            vmem((2, 2, 4, 4, 4, 16, PAIR), BF),
            vmem((2, 2, 3, 4, 4, 16, PAIR), BF),
            vmem((2, 2, 4, 4, 16, PAIR), BF),
            vmem((2, 2, 3, 4, 16, PAIR), BF),
            vmem((2, 4, 2, 16, PAIR), BF),
            vmem((2, 3, 2, 16, PAIR), BF),
            pltpu.SMEM((1,), F32),
            vmem((4, 8, 128), F32),
            vmem((3, 3, 8, 128), F32),
            dma((5,)),
            dma((3,)),
            dma((2, 2)),
            dma((2,)),
            dma((2, 2)),
            dma((2, 3)),
            dma((2, 3)),
            dma((2,)),
            dma((3,)),
            pltpu.SemaphoreType.REGULAR((2,)),
        ],
        compiler_params=pltpu.CompilerParams(collective_id=0, has_side_effects=True, vmem_limit_bytes=62 * 2**20),
    )(
        queries,
        keys,
        values,
        out_grad,
        ref_keys.reshape(4, 32, -1),
        ref_values.reshape(4, 32, -1),
        frame_weight,
    )
    return pl.pallas_call(
        hand_on,
        name="hand_on",
        out_shape=out_shape,
        in_specs=[pl.BlockSpec(memory_space=pltpu.VMEM)] * 5,
        out_specs=[hbm] * 5,
        scratch_shapes=[dma((5,))],
        compiler_params=pltpu.CompilerParams(vmem_limit_bytes=2**20),
    )(*grads)


def solution(mesh):
    tokens = P("frame", "ref")
    return jax.shard_map(
        per_device,
        mesh=mesh,
        in_specs=(tokens, tokens, tokens, tokens, P("ref", None), P("ref", None), P("frame")),
        out_specs=(tokens,) * 5,
        check_vma=False,
    )
```

```python
import jax
import jax.numpy as jnp
from jax import lax
from jax.experimental import pallas as pl
from jax.experimental.pallas import tpu as pltpu
from jax.sharding import PartitionSpec as P

F32, BF = jnp.float32, jnp.bfloat16
MESH = pl.DeviceIdType.MESH
SCALE = 0.125
EXP2_SCALE = SCALE * 1.4426950408889634
SEQ, WIDTH, PAIR = 256, 256, 128
FRAMES = 64
KEY, VALUE = 0, 1


def dot(a, b):
    return lax.dot_general(a, b, (((1,), (0,)), ((), ())), preferred_element_type=F32)


def fold(a):
    return jnp.sum(a.reshape(-1, 8, a.shape[-1]), axis=0)


def split_heads(p, a, stacked, across):
    a = a[:, PAIR * p : PAIR * (p + 1)]
    low = lax.broadcasted_iota(jnp.int32, (SEQ, PAIR), 1) < 64
    zero = jnp.zeros((SEQ, PAIR), BF)
    stacked[p, 0:SEQ] = jnp.where(low, a, zero)
    stacked[p, SEQ:] = jnp.where(low, zero, a)
    turned = a.T
    top = lax.broadcasted_iota(jnp.int32, (PAIR, SEQ), 0) < 64
    zero = jnp.zeros((PAIR, SEQ), BF)
    across[p, :, 0:SEQ] = jnp.where(top, turned, zero)
    across[p, :, SEQ:] = jnp.where(top, zero, turned)


def kernel(
    q_in, k_in, v_in, d_in, rk_in, rv_in, w_in,
    gq_out, gk_out, gv_out, grk_out, grv_out,
    own, refs, stacked, across, raised, gshare, gscore, gq_t, gkv,
    part, got1, part2, got2, part3, got3, own_weight, weights, weights_got,
    loc_sem, sent_sem, zr, cr, gr, r1, r2, r3, wr, hop_sem,
):
    frame, ref = lax.axis_index("frame"), lax.axis_index("ref")
    zhi, x, y = frame // 16, (frame // 4) % 4, frame % 4
    zlo, core = ref // 2, ref % 2

    def at(dx=0, dy=0, dz=0, c=core):
        z = (zhi * 4 + zlo + dz + 16) % 16
        return (((z // 4) * 4 + (x + dx) % 4) * 4 + (y + dy) % 4, (z % 4) * 2 + c)

    def signal(sem, device):
        pl.semaphore_signal(sem, inc=1, device_id=device, device_id_type=MESH)

    near = [at(c=1 - core)]
    near += [at(dz=dz, c=c) for dz in (1, -1, 2, -2) for c in (0, 1)]
    near += [at(dx=o) for o in (1, 2, 3)] + [at(dy=o) for o in (1, 2, 3)]
    barrier = pltpu.get_barrier_semaphore()
    for device in near:
        signal(barrier, device)

    def columns(r, h):
        return pl.ds(pl.multiple_of(r * WIDTH + h * PAIR, PAIR), PAIR)

    ref_in = (rk_in, rv_in)
    weight_copy = pltpu.make_async_copy(w_in, own_weight, loc_sem.at[0])
    weight_copy.start()
    for i, a in enumerate((q_in, d_in, k_in, v_in)):
        pltpu.make_async_copy(a, own.at[i], loc_sem.at[1 + i // 2]).start()
    for h in (0, 1):
        for t in (0, 1):
            pltpu.make_async_copy(ref_in[t].at[:, :, columns(ref, h)], refs.at[t, h, 0, core], loc_sem.at[3 + h]).start()

    def copied(region, sem):
        pltpu.make_async_copy(region, region, sem).wait()

    pl.semaphore_wait(barrier, len(near))
    for dz in (2, -2):
        signal(hop_sem.at[0], at(dz=dz))

    def send(src, dst, phase, recv_sem, device):
        pltpu.make_async_remote_copy(src, dst, sent_sem.at[phase], recv_sem, device_id=device, device_id_type=MESH).start()

    def arrived(region, sem):
        pltpu.make_async_remote_copy(region, region, sent_sem.at[0], sem, device_id=at(dx=1), device_id_type=MESH).wait_recv()

    def all_sent(region, phase):
        pltpu.make_async_remote_copy(region, region, sent_sem.at[phase], wr.at[0], device_id=at(dx=1), device_id_type=MESH).wait_send()

    quarter = (x, y)
    for h in (0, 1):
        for t in (0, 1):
            for c in (0, 1):
                target = at(dz=2 if t == 0 else -2, c=c)
                here = ref_in[t].at[quarter[t], :, columns(target[1], h)]
                send(here, refs.at[t, h, 3, core, quarter[t]], 0, zr.at[h, t], target)
    for h in (0, 1):
        for t in (0, 1):
            for dz, place in ((1, 2), (-1, 1)):
                for c in (0, 1):
                    target = at(dz=dz, c=c)
                    send(ref_in[t].at[:, :, columns(target[1], h)], refs.at[t, h, place, core], 0, gr.at[h, 0], target)
    weight_copy.wait()
    weight = own_weight[0]
    weights[0] = jnp.full((8, 128), weight, F32)
    for h in (0, 1):
        for t in (0, 1):
            here = ref_in[t].at[:, :, columns(zlo * 2 + 1 - core, h)]
            send(here, refs.at[t, h, 0, core], 0, cr.at[h], at(c=1 - core))
    for o in (1, 2, 3):
        send(weights.at[0], weights_got.at[0, o - 1], 2, wr.at[0], at(dx=o))

    def gather_planes(h):
        for t in (0, 1):
            mine = refs.at[t, h, 3, :, quarter[t]]
            arrived(mine, zr.at[h, t])
            for o in (2, 1, 3):
                send(mine, mine, 0, gr.at[h, 1], at(dx=o) if t == 0 else at(dy=o))

    def wait_adjacent(h):
        arrived(refs.at[:, h, 1:3], gr.at[h, 0])

    def wait_planes(h):
        arrived(refs.at[:, h, 3, :, 0:3], gr.at[h, 1])

    totals = [None, None]

    def scores(p, j, keys, values):
        e = jnp.exp2(dot(keys, across[0, p]) * EXP2_SCALE)
        g = dot(values, across[1, p])
        raised[p, j] = e
        gshare[p, j] = g
        more = (fold(e), fold(e * g))
        totals[p] = more if totals[p] is None else (totals[p][0] + more[0], totals[p][1] + more[1])

    def ref_chunk(t, p, s):
        return refs[t, p, s].reshape(SEQ, PAIR)

    def ref_scores(p, s):
        scores(p, s, ref_chunk(0, p, s), ref_chunk(1, p, s))

    def own_chunk(i, p):
        return own[i, :, PAIR * p : PAIR * (p + 1)]

    def weight_stage(stage):
        arrived(weights_got.at[stage], wr.at[stage])
        weights[stage + 1] = weights[stage] + weights_got[stage, 0] + weights_got[stage, 1] + weights_got[stage, 2]
        if stage < 2:
            for o in (1, 2, 3):
                target = at(dy=o) if stage == 0 else at(dz=4 * o)
                send(weights.at[stage + 1], weights_got.at[stage + 1, o - 1], 2, wr.at[stage + 1], target)

    copied(own.at[0:2], loc_sem.at[1])
    for p in (0, 1):
        split_heads(p, own[0], stacked.at[0], across.at[0])
        split_heads(p, own[1], stacked.at[1], across.at[1])
    copied(own.at[2:4], loc_sem.at[2])
    scores(0, 4, own_chunk(2, 0), own_chunk(3, 0))
    scores(1, 4, own_chunk(2, 1), own_chunk(3, 1))
    gather_planes(0)
    gather_planes(1)
    pl.semaphore_wait(hop_sem.at[0], 2)
    for dz in (4, -4):
        signal(hop_sem.at[1], at(dz=dz))
    weight_stage(0)
    for h in (0, 1):
        copied(refs.at[:, h, 0, core], loc_sem.at[3 + h])
        arrived(refs.at[:, h, 0, 1 - core], cr.at[h])
        ref_scores(h, 0)

    def shares(p, j, norm):
        share = raised[p, j] * norm[0]
        score = (share * (gshare[p, j] - norm[1])).astype(BF)
        gscore[p, j] = score
        return dot(score, stacked[0, p]), dot(share.astype(BF), stacked[1, p])

    norms = [None, None]

    def normalise(p):
        norm = 1.0 / jnp.sum(totals[p][0], axis=0, keepdims=True)
        norms[p] = (norm, jnp.sum(totals[p][1], axis=0, keepdims=True) * norm)

    order = (2, 1, 3, 0)
    parts = ((0, 1), (1, 3), (3, 4))

    def first_stage(p, group):
        first, last = parts[group]
        for i in range(first, last):
            step = (zhi + order[i] - zlo + 4) % 4
            place = step + (step // 2) * (5 - 2 * step)
            for t, grad in enumerate(shares(p, place, norms[p])):
                part[t, p, i] = (grad * weight).astype(BF).reshape(4, 4, 16, PAIR)

    def first_send(p, group):
        first, last = parts[group]
        for o in (2, 1, 3):
            for t in (0, 1):
                here = part.at[0, p, first:last, (x + o) % 4] if t == 0 else part.at[1, p, first:last, :, (y + o) % 4]
                send(here, got1.at[t, p, o - 1, first:last], 1, r1.at[p, group], at(dx=o) if t == 0 else at(dy=o))

    def total(first, got):
        return first.astype(F32) + got[0].astype(F32) + got[1].astype(F32) + got[2].astype(F32)

    def second_stage(p, group):
        first, last = parts[group]
        arrived(got1.at[:, p, :, first:last], r1.at[p, group])
        for t in (0, 1):
            mine = part[0, p, first:last, x] if t == 0 else part[1, p, first:last, :, y]
            part2[t, p, first:last] = total(mine, got1[t, p, :, first:last]).astype(BF)
            for o in (2, 1, 3):
                here = part2.at[t, p, first:last, (y + o) % 4 if t == 0 else (x + o) % 4]
                send(here, got2.at[t, p, o - 1, first:last], 1, r2.at[p, group], at(dy=o) if t == 0 else at(dx=o))

    def third_stage(p, group):
        first, last = parts[group]
        arrived(got2.at[:, p, :, first:last], r2.at[p, group])
        for t in (0, 1):
            part3[p, first:last, t] = total(part2[t, p, first:last, y if t == 0 else x], got2[t, p, :, first:last]).astype(BF)
        for i in range(first, min(last, 3)):
            send(part3.at[p, i], got3.at[p, i], 1, r3.at[p], at(dz=4 * order[i]))

    def frame_grads(p):
        gk, gv = shares(p, 4, norms[p])
        gkv[0, p] = gk
        gkv[1, p] = gv
        sums = [None, None]
        for j in range(5):
            turned = (own_chunk(2, p) if j == 4 else ref_chunk(0, p, j)).T
            for a in (0, 1):
                more = dot(turned[64 * a : 64 * (a + 1)], gscore[p, j, :, SEQ * a : SEQ * (a + 1)])
                sums[a] = more if sums[a] is None else sums[a] + more
        gq_t[p, 0:64] = sums[0]
        gq_t[p, 64:128] = sums[1]

    wait_adjacent(0)
    ref_scores(0, 1)
    ref_scores(0, 2)
    wait_planes(0)
    ref_scores(0, 3)
    normalise(0)
    first_stage(0, 0)
    first_send(0, 0)
    first_stage(0, 1)
    first_send(0, 1)
    first_stage(0, 2)
    wait_planes(1)
    ref_scores(1, 3)
    wait_adjacent(1)
    ref_scores(1, 1)
    ref_scores(1, 2)
    normalise(1)
    first_stage(1, 0)
    first_send(1, 0)
    first_stage(1, 1)
    first_send(1, 1)
    first_send(0, 2)
    first_stage(1, 2)
    first_send(1, 2)
    pl.semaphore_wait(hop_sem.at[1], 2)
    weight_stage(1)
    second_stage(0, 0)
    second_stage(0, 1)
    second_stage(1, 0)
    second_stage(1, 1)
    third_stage(0, 0)
    second_stage(0, 2)
    second_stage(1, 2)
    third_stage(1, 0)
    third_stage(0, 1)
    third_stage(1, 1)
    frame_grads(0)
    frame_grads(1)
    third_stage(0, 2)
    third_stage(1, 2)
    weight_stage(2)
    factor = FRAMES / weights[3, 0:1, 0:1]
    own_factor = weight * factor
    for p in (0, 1):
        cols = slice(PAIR * p, PAIR * (p + 1))
        gq_out[:, cols] = (gq_t[p].T * (own_factor * SCALE)).astype(BF)
        gk_out[:, cols] = (gkv[0, p] * (own_factor * SCALE)).astype(BF)
        gv_out[:, cols] = (gkv[1, p] * own_factor).astype(BF)
    all_sent(raised.at[0, 0:2, 0:224], 0)
    all_sent(raised.at[0, 0:3, 0:168], 1)
    all_sent(weights_got, 2)
    for p in (0, 1):
        arrived(got3.at[p], r3.at[p])
        sums = total(part3[p, 3], got3[p])
        grk_out[:, PAIR * p : PAIR * (p + 1)] = sums[0] * (factor * SCALE)
        grv_out[:, PAIR * p : PAIR * (p + 1)] = sums[1] * factor


def hand_on(*refs):
    copies = [pltpu.make_async_copy(refs[i], refs[5 + i], refs[10].at[i]) for i in range(5)]
    for copy in copies:
        copy.start()
    for copy in copies:
        copy.wait()


def per_device(queries, keys, values, out_grad, ref_keys, ref_values, frame_weight):
    hbm = pl.BlockSpec(memory_space=pl.ANY)
    shape = jax.ShapeDtypeStruct
    vmem, dma = pltpu.VMEM, pltpu.SemaphoreType.DMA
    out_shape = (shape((SEQ, WIDTH), BF),) * 3 + (shape((16, WIDTH), F32),) * 2
    grads = pl.pallas_call(
        kernel,
        name="joint_attention_grads",
        out_shape=tuple(pltpu.VMEM(a.shape, a.dtype) for a in out_shape),
        in_specs=[hbm] * 7,
        out_specs=[pl.BlockSpec(memory_space=pltpu.VMEM)] * 5,
        scratch_shapes=[
            vmem((4, SEQ, WIDTH), BF),
            vmem((2, 2, 4, 2, 4, 32, PAIR), BF),
            vmem((2, 2, 2 * SEQ, PAIR), BF),
            vmem((2, 2, PAIR, 2 * SEQ), BF),
            vmem((2, 5, SEQ, 2 * SEQ), F32),
            vmem((2, 5, SEQ, 2 * SEQ), F32),
            vmem((2, 5, SEQ, 2 * SEQ), BF),
            vmem((2, PAIR, SEQ), F32),
            vmem((2, 2, SEQ, PAIR), F32),
            vmem((2, 2, 4, 4, 4, 16, PAIR), BF),
            vmem((2, 2, 3, 4, 4, 16, PAIR), BF),
            vmem((2, 2, 4, 4, 16, PAIR), BF),
            vmem((2, 2, 3, 4, 16, PAIR), BF),
            vmem((2, 4, 2, 16, PAIR), BF),
            vmem((2, 3, 2, 16, PAIR), BF),
            pltpu.SMEM((1,), F32),
            vmem((4, 8, 128), F32),
            vmem((3, 3, 8, 128), F32),
            dma((5,)),
            dma((3,)),
            dma((2, 2)),
            dma((2,)),
            dma((2, 2)),
            dma((2, 3)),
            dma((2, 3)),
            dma((2,)),
            dma((3,)),
            pltpu.SemaphoreType.REGULAR((2,)),
        ],
        compiler_params=pltpu.CompilerParams(collective_id=0, has_side_effects=True, vmem_limit_bytes=62 * 2**20),
    )(
        queries,
        keys,
        values,
        out_grad,
        ref_keys.reshape(4, 32, -1),
        ref_values.reshape(4, 32, -1),
        frame_weight,
    )
    return pl.pallas_call(
        hand_on,
        name="hand_on",
        out_shape=out_shape,
        in_specs=[pl.BlockSpec(memory_space=pltpu.VMEM)] * 5,
        out_specs=[hbm] * 5,
        scratch_shapes=[dma((5,))],
        compiler_params=pltpu.CompilerParams(vmem_limit_bytes=2**20),
    )(*grads)


def solution(mesh):
    tokens = P("frame", "ref")
    return jax.shard_map(
        per_device,
        mesh=mesh,
        in_specs=(tokens, tokens, tokens, tokens, P("ref", None), P("ref", None), P("frame")),
        out_specs=(tokens,) * 5,
        check_vma=False,
    )
```

```python
import jax
import jax.numpy as jnp
from jax import lax
from jax.experimental import pallas as pl
from jax.experimental.pallas import tpu as pltpu
from jax.sharding import PartitionSpec as P

F32, BF = jnp.float32, jnp.bfloat16
MESH = pl.DeviceIdType.MESH
SCALE = 0.125
EXP2_SCALE = SCALE * 1.4426950408889634
SEQ, WIDTH, PAIR = 256, 256, 128
FRAMES = 64
KEY, VALUE = 0, 1


def dot(a, b):
    return lax.dot_general(a, b, (((1,), (0,)), ((), ())), preferred_element_type=F32)


def fold(a):
    return jnp.sum(a.reshape(-1, 8, a.shape[-1]), axis=0)


def split_heads(p, a, stacked, across):
    a = a[:, PAIR * p : PAIR * (p + 1)]
    low = lax.broadcasted_iota(jnp.int32, (SEQ, PAIR), 1) < 64
    zero = jnp.zeros((SEQ, PAIR), BF)
    stacked[p, 0:SEQ] = jnp.where(low, a, zero)
    stacked[p, SEQ:] = jnp.where(low, zero, a)
    turned = a.T
    top = lax.broadcasted_iota(jnp.int32, (PAIR, SEQ), 0) < 64
    zero = jnp.zeros((PAIR, SEQ), BF)
    across[p, :, 0:SEQ] = jnp.where(top, turned, zero)
    across[p, :, SEQ:] = jnp.where(top, zero, turned)


def kernel(
    q_in, k_in, v_in, d_in, rk_in, rv_in, w_in,
    gq_out, gk_out, gv_out, grk_out, grv_out,
    own, refs, stacked, across, raised, gshare, gscore, gq_t, gkv,
    part, got1, part2, got2, part3, got3, own_weight, weights, weights_got,
    loc_sem, sent_sem, zr, cr, gr, r1, r2, r3, wr, hop_sem,
):
    frame, ref = lax.axis_index("frame"), lax.axis_index("ref")
    zhi, x, y = frame // 16, (frame // 4) % 4, frame % 4
    zlo, core = ref // 2, ref % 2

    def at(dx=0, dy=0, dz=0, c=core):
        z = (zhi * 4 + zlo + dz + 16) % 16
        return (((z // 4) * 4 + (x + dx) % 4) * 4 + (y + dy) % 4, (z % 4) * 2 + c)

    def signal(sem, device):
        pl.semaphore_signal(sem, inc=1, device_id=device, device_id_type=MESH)

    near = [at(c=1 - core)]
    near += [at(dz=dz, c=c) for dz in (1, -1, 2, -2) for c in (0, 1)]
    near += [at(dx=o) for o in (1, 2, 3)] + [at(dy=o) for o in (1, 2, 3)]
    barrier = pltpu.get_barrier_semaphore()
    for device in near:
        signal(barrier, device)

    def columns(r, h):
        return pl.ds(pl.multiple_of(r * WIDTH + h * PAIR, PAIR), PAIR)

    ref_in = (rk_in, rv_in)
    weight_copy = pltpu.make_async_copy(w_in, own_weight, loc_sem.at[0])
    weight_copy.start()
    for i, a in enumerate((q_in, d_in, k_in, v_in)):
        pltpu.make_async_copy(a, own.at[i], loc_sem.at[1 + i // 2]).start()
    for h in (0, 1):
        for t in (0, 1):
            pltpu.make_async_copy(ref_in[t].at[:, :, columns(ref, h)], refs.at[t, h, 0, core], loc_sem.at[3 + h]).start()

    def copied(region, sem):
        pltpu.make_async_copy(region, region, sem).wait()

    pl.semaphore_wait(barrier, len(near))
    for dz in (2, -2):
        signal(hop_sem.at[0], at(dz=dz))

    def send(src, dst, phase, recv_sem, device):
        pltpu.make_async_remote_copy(src, dst, sent_sem.at[phase], recv_sem, device_id=device, device_id_type=MESH).start()

    def arrived(region, sem):
        pltpu.make_async_remote_copy(region, region, sent_sem.at[0], sem, device_id=at(dx=1), device_id_type=MESH).wait_recv()

    def all_sent(region, phase):
        pltpu.make_async_remote_copy(region, region, sent_sem.at[phase], wr.at[0], device_id=at(dx=1), device_id_type=MESH).wait_send()

    quarter = (x, y)
    for h in (0, 1):
        for t in (0, 1):
            for c in (0, 1):
                target = at(dz=2 if t == 0 else -2, c=c)
                here = ref_in[t].at[quarter[t], :, columns(target[1], h)]
                send(here, refs.at[t, h, 3, core, quarter[t]], 0, zr.at[h, t], target)
    for h in (0, 1):
        for t in (0, 1):
            for dz, place in ((1, 2), (-1, 1)):
                for c in (0, 1):
                    target = at(dz=dz, c=c)
                    send(ref_in[t].at[:, :, columns(target[1], h)], refs.at[t, h, place, core], 0, gr.at[h, 0], target)
    weight_copy.wait()
    weight = own_weight[0]
    weights[0] = jnp.full((8, 128), weight, F32)
    for h in (0, 1):
        for t in (0, 1):
            here = ref_in[t].at[:, :, columns(zlo * 2 + 1 - core, h)]
            send(here, refs.at[t, h, 0, core], 0, cr.at[h], at(c=1 - core))
    for o in (1, 2, 3):
        send(weights.at[0], weights_got.at[0, o - 1], 2, wr.at[0], at(dx=o))

    def gather_planes(h):
        for t in (0, 1):
            mine = refs.at[t, h, 3, :, quarter[t]]
            arrived(mine, zr.at[h, t])
            for o in (2, 1, 3):
                send(mine, mine, 0, gr.at[h, 1], at(dx=o) if t == 0 else at(dy=o))

    def wait_adjacent(h):
        arrived(refs.at[:, h, 1:3], gr.at[h, 0])

    def wait_planes(h):
        arrived(refs.at[:, h, 3, :, 0:3], gr.at[h, 1])

    totals = [None, None]

    def scores(p, j, keys, values):
        e = jnp.exp2(dot(keys, across[0, p]) * EXP2_SCALE)
        g = dot(values, across[1, p])
        raised[p, j] = e
        gshare[p, j] = g
        more = (fold(e), fold(e * g))
        totals[p] = more if totals[p] is None else (totals[p][0] + more[0], totals[p][1] + more[1])

    def ref_chunk(t, p, s):
        return refs[t, p, s].reshape(SEQ, PAIR)

    def ref_scores(p, s):
        scores(p, s, ref_chunk(0, p, s), ref_chunk(1, p, s))

    def own_chunk(i, p):
        return own[i, :, PAIR * p : PAIR * (p + 1)]

    def weight_stage(stage):
        arrived(weights_got.at[stage], wr.at[stage])
        weights[stage + 1] = weights[stage] + weights_got[stage, 0] + weights_got[stage, 1] + weights_got[stage, 2]
        if stage < 2:
            for o in (1, 2, 3):
                target = at(dy=o) if stage == 0 else at(dz=4 * o)
                send(weights.at[stage + 1], weights_got.at[stage + 1, o - 1], 2, wr.at[stage + 1], target)

    copied(own.at[0:2], loc_sem.at[1])
    for p in (0, 1):
        split_heads(p, own[0], stacked.at[0], across.at[0])
        split_heads(p, own[1], stacked.at[1], across.at[1])
    copied(own.at[2:4], loc_sem.at[2])
    scores(0, 4, own_chunk(2, 0), own_chunk(3, 0))
    scores(1, 4, own_chunk(2, 1), own_chunk(3, 1))
    gather_planes(0)
    gather_planes(1)
    pl.semaphore_wait(hop_sem.at[0], 2)
    for dz in (4, -4):
        signal(hop_sem.at[1], at(dz=dz))
    weight_stage(0)
    for h in (0, 1):
        copied(refs.at[:, h, 0, core], loc_sem.at[3 + h])
        arrived(refs.at[:, h, 0, 1 - core], cr.at[h])
        ref_scores(h, 0)

    def shares(p, j, norm):
        share = raised[p, j] * norm[0]
        score = (share * (gshare[p, j] - norm[1])).astype(BF)
        gscore[p, j] = score
        return dot(score, stacked[0, p]), dot(share.astype(BF), stacked[1, p])

    norms = [None, None]

    def normalise(p):
        norm = 1.0 / jnp.sum(totals[p][0], axis=0, keepdims=True)
        norms[p] = (norm, jnp.sum(totals[p][1], axis=0, keepdims=True) * norm)

    order = (2, 1, 3, 0)
    parts = ((0, 1), (1, 3), (3, 4))

    def first_stage(p, group):
        first, last = parts[group]
        for i in range(first, last):
            step = (zhi + order[i] - zlo + 4) % 4
            place = step + (step // 2) * (5 - 2 * step)
            for t, grad in enumerate(shares(p, place, norms[p])):
                part[t, p, i] = (grad * weight).astype(BF).reshape(4, 4, 16, PAIR)

    def first_send(p, group):
        first, last = parts[group]
        for o in (2, 1, 3):
            for t in (0, 1):
                here = part.at[0, p, first:last, (x + o) % 4] if t == 0 else part.at[1, p, first:last, :, (y + o) % 4]
                send(here, got1.at[t, p, o - 1, first:last], 1, r1.at[p, group], at(dx=o) if t == 0 else at(dy=o))

    def total(first, got):
        return first.astype(F32) + got[0].astype(F32) + got[1].astype(F32) + got[2].astype(F32)

    def second_stage(p, group):
        first, last = parts[group]
        arrived(got1.at[:, p, :, first:last], r1.at[p, group])
        for t in (0, 1):
            mine = part[0, p, first:last, x] if t == 0 else part[1, p, first:last, :, y]
            part2[t, p, first:last] = total(mine, got1[t, p, :, first:last]).astype(BF)
            for o in (2, 1, 3):
                here = part2.at[t, p, first:last, (y + o) % 4 if t == 0 else (x + o) % 4]
                send(here, got2.at[t, p, o - 1, first:last], 1, r2.at[p, group], at(dy=o) if t == 0 else at(dx=o))

    def third_stage(p, group):
        first, last = parts[group]
        arrived(got2.at[:, p, :, first:last], r2.at[p, group])
        for t in (0, 1):
            part3[p, first:last, t] = total(part2[t, p, first:last, y if t == 0 else x], got2[t, p, :, first:last]).astype(BF)
        for i in range(first, min(last, 3)):
            send(part3.at[p, i], got3.at[p, i], 1, r3.at[p], at(dz=4 * order[i]))

    def frame_grads(p):
        gk, gv = shares(p, 4, norms[p])
        gkv[0, p] = gk
        gkv[1, p] = gv
        sums = [None, None]
        for j in range(5):
            turned = (own_chunk(2, p) if j == 4 else ref_chunk(0, p, j)).T
            for a in (0, 1):
                more = dot(turned[64 * a : 64 * (a + 1)], gscore[p, j, :, SEQ * a : SEQ * (a + 1)])
                sums[a] = more if sums[a] is None else sums[a] + more
        gq_t[p, 0:64] = sums[0]
        gq_t[p, 64:128] = sums[1]

    wait_adjacent(0)
    ref_scores(0, 1)
    ref_scores(0, 2)
    wait_planes(0)
    ref_scores(0, 3)
    normalise(0)
    first_stage(0, 0)
    first_send(0, 0)
    first_stage(0, 1)
    first_send(0, 1)
    first_stage(0, 2)
    wait_planes(1)
    ref_scores(1, 3)
    wait_adjacent(1)
    ref_scores(1, 1)
    ref_scores(1, 2)
    normalise(1)
    first_stage(1, 0)
    first_send(1, 0)
    first_stage(1, 1)
    first_send(1, 1)
    first_stage(1, 2)
    pl.semaphore_wait(hop_sem.at[1], 2)
    weight_stage(1)
    second_stage(0, 0)
    second_stage(0, 1)
    second_stage(1, 0)
    first_send(0, 2)
    first_send(1, 2)
    second_stage(1, 1)
    third_stage(0, 0)
    third_stage(1, 0)
    third_stage(0, 1)
    second_stage(0, 2)
    second_stage(1, 2)
    third_stage(1, 1)
    frame_grads(0)
    frame_grads(1)
    third_stage(0, 2)
    third_stage(1, 2)
    weight_stage(2)
    factor = FRAMES / weights[3, 0:1, 0:1]
    own_factor = weight * factor
    for p in (0, 1):
        cols = slice(PAIR * p, PAIR * (p + 1))
        gq_out[:, cols] = (gq_t[p].T * (own_factor * SCALE)).astype(BF)
        gk_out[:, cols] = (gkv[0, p] * (own_factor * SCALE)).astype(BF)
        gv_out[:, cols] = (gkv[1, p] * own_factor).astype(BF)
    all_sent(raised.at[0, 0:2, 0:224], 0)
    all_sent(raised.at[0, 0:3, 0:168], 1)
    all_sent(weights_got, 2)
    for p in (0, 1):
        arrived(got3.at[p], r3.at[p])
        sums = total(part3[p, 3], got3[p])
        grk_out[:, PAIR * p : PAIR * (p + 1)] = sums[0] * (factor * SCALE)
        grv_out[:, PAIR * p : PAIR * (p + 1)] = sums[1] * factor


def hand_on(*refs):
    copies = [pltpu.make_async_copy(refs[i], refs[5 + i], refs[10].at[i]) for i in range(5)]
    for copy in copies:
        copy.start()
    for copy in copies:
        copy.wait()


def per_device(queries, keys, values, out_grad, ref_keys, ref_values, frame_weight):
    hbm = pl.BlockSpec(memory_space=pl.ANY)
    shape = jax.ShapeDtypeStruct
    vmem, dma = pltpu.VMEM, pltpu.SemaphoreType.DMA
    out_shape = (shape((SEQ, WIDTH), BF),) * 3 + (shape((16, WIDTH), F32),) * 2
    grads = pl.pallas_call(
        kernel,
        name="joint_attention_grads",
        out_shape=tuple(pltpu.VMEM(a.shape, a.dtype) for a in out_shape),
        in_specs=[hbm] * 7,
        out_specs=[pl.BlockSpec(memory_space=pltpu.VMEM)] * 5,
        scratch_shapes=[
            vmem((4, SEQ, WIDTH), BF),
            vmem((2, 2, 4, 2, 4, 32, PAIR), BF),
            vmem((2, 2, 2 * SEQ, PAIR), BF),
            vmem((2, 2, PAIR, 2 * SEQ), BF),
            vmem((2, 5, SEQ, 2 * SEQ), F32),
            vmem((2, 5, SEQ, 2 * SEQ), F32),
            vmem((2, 5, SEQ, 2 * SEQ), BF),
            vmem((2, PAIR, SEQ), F32),
            vmem((2, 2, SEQ, PAIR), F32),
            vmem((2, 2, 4, 4, 4, 16, PAIR), BF),
            vmem((2, 2, 3, 4, 4, 16, PAIR), BF),
            vmem((2, 2, 4, 4, 16, PAIR), BF),
            vmem((2, 2, 3, 4, 16, PAIR), BF),
            vmem((2, 4, 2, 16, PAIR), BF),
            vmem((2, 3, 2, 16, PAIR), BF),
            pltpu.SMEM((1,), F32),
            vmem((4, 8, 128), F32),
            vmem((3, 3, 8, 128), F32),
            dma((5,)),
            dma((3,)),
            dma((2, 2)),
            dma((2,)),
            dma((2, 2)),
            dma((2, 3)),
            dma((2, 3)),
            dma((2,)),
            dma((3,)),
            pltpu.SemaphoreType.REGULAR((2,)),
        ],
        compiler_params=pltpu.CompilerParams(collective_id=0, has_side_effects=True, vmem_limit_bytes=62 * 2**20),
    )(
        queries,
        keys,
        values,
        out_grad,
        ref_keys.reshape(4, 32, -1),
        ref_values.reshape(4, 32, -1),
        frame_weight,
    )
    return pl.pallas_call(
        hand_on,
        name="hand_on",
        out_shape=out_shape,
        in_specs=[pl.BlockSpec(memory_space=pltpu.VMEM)] * 5,
        out_specs=[hbm] * 5,
        scratch_shapes=[dma((5,))],
        compiler_params=pltpu.CompilerParams(vmem_limit_bytes=2**20),
    )(*grads)


def solution(mesh):
    tokens = P("frame", "ref")
    return jax.shard_map(
        per_device,
        mesh=mesh,
        in_specs=(tokens, tokens, tokens, tokens, P("ref", None), P("ref", None), P("frame")),
        out_specs=(tokens,) * 5,
        check_vma=False,
    )
```
